32 devices in a mesh: dp: 4 (over x, core), feat: 8 (over z, y).
Axes of the slice: x: 2, y: 2, z: 4, core: 2. Of those that a mesh axis runs over, the one named last changes fastest.
Arguments:
- features: bfloat16 [6144, 65536], P('dp', 'feat'), may hold values from -64 to 64
- weight: float32 [16, 65536], P(None, 'feat'), may hold values from -1 to 1
- labels: int32 [6144], P('dp'), may hold values from 0 to 15
- sample_weight: int32 [6144], P('dp'), may hold values from 1 to 4
Outputs:
- logit_step: float32 [6144, 16], P('dp')
- mean_loss: float32 [], replicated
The draws below stay inside these ranges and needn't reach their ends.
All inputs are finite; a program needn't handle non-finite values.
Results may differ from the reference program's by a relative error of at most 0.014.
Values may be sent and summed in bfloat16 or wider, within the bound.
No kernel may reach another device: no remote copies, remote signals or barrier semaphores. Data moves between devices by JAX's collectives and lax.ppermute only.
A program may use at most 64 MiB of HBM per device.

```python
import math
import jax
import jax.numpy as jnp

K = 16
CG_ITERS = 4
F = 65536
ROWS = 6144


def draw_weight(key, part):
    normal_part = jax.random.normal(jax.random.fold_in(key, 11), (K, F), dtype=jnp.float32)
    return jnp.clip(normal_part, -4.0, 4.0) * (1.0 / math.sqrt(F))


def draw_features(key, part):
    row_count = ROWS
    row_pos = (jnp.arange(row_count, dtype=jnp.float32) / row_count)[:, None]
    col_pos = (jnp.arange(F, dtype=jnp.float32) / F)[None, :]
    row_scale = jnp.exp(jax.random.uniform(jax.random.fold_in(key, 21), (row_count, 1), jnp.float32, math.log(0.3), math.log(3.0)))
    col_scale = jnp.exp(jax.random.uniform(jax.random.fold_in(key, 22), (1, F), jnp.float32, math.log(0.3), math.log(3.0)))
    ramps = jnp.exp((row_pos - 0.5) * math.log(3.0)) * jnp.exp((col_pos - 0.5) * math.log(3.0))
    normal_part = jnp.clip(jax.random.normal(jax.random.fold_in(key, 29), (row_count, F), dtype=jnp.float32), -4.0, 4.0)
    values = normal_part * row_scale * col_scale * ramps
    return jnp.clip(values, -64.0, 64.0).astype(jnp.bfloat16)


def with_ends(array, stream_key, smallest, high):
    longest = array.shape.index(max(array.shape))
    spots = []
    for shift in (0, 1):
        where = [jax.random.randint(jax.random.fold_in(stream_key, axis), (), 0, length) for axis, length in enumerate(array.shape)]
        where[longest] = (where[longest] + shift) % array.shape[longest]
        spots.append(tuple(where))
    return array.at[spots[0]].set(smallest).at[spots[1]].set(high)


def setup_inputs(seed: int = 0) -> dict:
    splits = jax.random.split(jax.random.key(seed), 5)
    features = draw_features(jax.random.fold_in(splits[4], 71), 0)
    weight = draw_weight(jax.random.fold_in(splits[4], 71), 0)
    labels = with_ends(jax.random.randint(splits[2], (ROWS,), 0, K), jax.random.fold_in(splits[2], 1), 0, K - 1).astype(jnp.int32)
    sample_weight = with_ends(jax.random.randint(splits[3], (ROWS,), 1, 5), jax.random.fold_in(splits[3], 1), 1, 4).astype(jnp.int32)
    return {"features": features, "weight": weight, "labels": labels, "sample_weight": sample_weight}


RIDGE_COEF = 0.1
NORM_GUARD = 1e-6


def reference(features, weight, labels, sample_weight):
    weight_b = weight.astype(jnp.bfloat16)
    logits = jnp.dot(features, weight_b.T, preferred_element_type=jnp.float32)
    row_top = jnp.max(logits, axis=1, keepdims=True)
    shifted = jnp.exp(logits - row_top)
    summed = jnp.sum(shifted, axis=1, keepdims=True)
    class_prob = shifted / summed
    log_total = row_top[:, 0] + jnp.log(summed[:, 0])
    row_weight = sample_weight.astype(jnp.float32)
    weight_total = jnp.sum(row_weight)
    onehot = (labels[:, None] == jnp.arange(K, dtype=jnp.int32)[None, :]).astype(jnp.float32)
    picked = jnp.sum(logits * onehot, axis=1)
    mean_loss = jnp.sum(row_weight * (log_total - picked)) / weight_total
    row_scale = (row_weight / weight_total)[:, None]
    resid_rows = (row_scale * (class_prob - onehot)).astype(jnp.bfloat16)
    gradient = jnp.dot(resid_rows.T, features, preferred_element_type=jnp.float32) + RIDGE_COEF * weight
    newton_step = jnp.zeros_like(gradient)
    residual = -gradient
    direction = residual
    res_norm = jnp.sum(residual * residual)
    for _ in range(CG_ITERS):
        direction_b = direction.astype(jnp.bfloat16)
        dir_scores = jnp.dot(features, direction_b.T, preferred_element_type=jnp.float32)
        mixed_mean = jnp.sum(class_prob * dir_scores, axis=1, keepdims=True)
        curv_rows = (row_scale * class_prob * (dir_scores - mixed_mean)).astype(jnp.bfloat16)
        hess_image = jnp.dot(curv_rows.T, features, preferred_element_type=jnp.float32) + RIDGE_COEF * direction
        step_size = res_norm / jnp.sum(direction * hess_image)
        newton_step = newton_step + step_size * direction
        residual = residual - step_size * hess_image
        new_norm = jnp.sum(residual * residual)
        direction = residual + (new_norm / (res_norm + NORM_GUARD)) * direction
        res_norm = new_norm
    step_b = newton_step.astype(jnp.bfloat16)
    logit_step = jnp.dot(features, step_b.T, preferred_element_type=jnp.float32)
    return logit_step, mean_loss
```

```python
import functools

import jax
import jax.numpy as jnp
from jax import lax
from jax.sharding import PartitionSpec as P
import jax.experimental.pallas as pl
import jax.experimental.pallas.tpu as pltpu

CG_ITERS = 4
RIDGE_COEF = 0.1
NORM_GUARD = 1e-06
LANES = 128
VMEM_LIMIT = 8 * 2**20

F32 = jnp.float32
BF16 = jnp.bfloat16
NT = (((1,), (1,)), ((), ()))
NN = (((1,), (0,)), ((), ()))


def scalar_block(values, lane):
    rows = lax.broadcasted_iota(jnp.int32, (16, LANES), 0)
    lanes = lax.broadcasted_iota(jnp.int32, (16, LANES), 1)
    block = jnp.zeros((16, LANES), F32)
    for i, value in enumerate(values):
        rest = jnp.broadcast_to(value, (16, LANES))
        for part in range(3):
            piece = rest.astype(BF16).astype(F32)
            block = jnp.where(rows == 3 * i + part, piece, block)
            rest = rest - piece
    return jnp.where(lanes == lane, block, 0.0)


def read_scalar(block, i):
    rows = lax.broadcasted_iota(jnp.int32, (16, LANES), 0)
    mine = (rows >= 3 * i) & (rows < 3 * i + 3)
    return jnp.sum(jnp.where(mine, block, 0.0), keepdims=True)


def sum_all(value):
    return jnp.sum(value, keepdims=True)


def add_up(parts):
    values = [p[...].astype(F32) for p in parts]
    while len(values) > 1:
        values = [a + b for a, b in zip(values[::2], values[1::2])]
    return values[0]


def my_core():
    return lax.rem(lax.axis_index("dp"), 2)


def half_columns(x_ref, which, step, i):
    half = x_ref.shape[1] // 2
    return pl.ds(pl.multiple_of(which * half + i * step, LANES), step)


def load_kernel(x_hbm, w_ref, x_ref, l_ref, sems, *, chunks, ahead):
    step = x_ref.shape[0] // chunks

    def copy(i):
        rows = pl.ds(i * step, step)
        return pltpu.make_async_copy(x_hbm.at[rows], x_ref.at[rows], sems.at[i])

    for i in range(min(ahead, chunks)):
        copy(i).start()
    w = w_ref[...].astype(BF16)
    for i in range(chunks):
        copy(i).wait()
        if i + ahead < chunks:
            copy(i + ahead).start()
        rows = slice(i * step, (i + 1) * step)
        l_ref[:, rows] = lax.dot_general(w, x_ref[rows, :], NT, preferred_element_type=F32)


def column_half(c, x_ref, which, out_ref, step=1024):
    half = x_ref.shape[1] // 2
    step = min(step, half)
    for i in range(half // step):
        block = lax.dot_general(
            c, x_ref[:, half_columns(x_ref, which, step, i)], NN, preferred_element_type=F32
        )
        out_ref[:, i * step : (i + 1) * step] = block.astype(out_ref.dtype)


def probs_kernel(*refs, n):
    parts, (labels_ref, weight_ref, x_ref, p_ref, e_ref, send_ref, block_ref) = refs[:n], refs[n:]
    logits = add_up(parts)
    classes = logits.shape[0]
    top = jnp.max(logits, axis=0, keepdims=True)
    shifted = jnp.exp(logits - top)
    summed = jnp.sum(shifted, axis=0, keepdims=True)
    prob = shifted / summed
    log_total = top + jnp.log(summed)
    row_weight = weight_ref[...].astype(F32)
    rows = lax.broadcasted_iota(jnp.int32, logits.shape, 0)
    onehot = (rows == labels_ref[...]).astype(F32)
    picked = jnp.sum(logits * onehot, axis=0, keepdims=True)
    p_ref[...] = prob
    e = (row_weight * (prob - onehot)).astype(BF16)
    e_ref[...] = e
    block = scalar_block(
        (sum_all(row_weight), sum_all(row_weight * (log_total - picked))), lax.axis_index("dp")
    )
    half = x_ref.shape[1] // 2
    block_ref[...] = block
    send_ref[:, half:] = block.astype(BF16)
    column_half(e, x_ref, 1 - my_core(), send_ref)


def curvature(parts, s_prev, sc_prev, p_ref, scale_ref):
    total = add_up(parts)
    rows = p_ref.shape[1]
    block = total[:, rows:]
    u = total[:, :rows]
    res_norm = read_scalar(block, 0)
    if s_prev is None:
        beta = jnp.zeros((1, 1), F32)
        s = u
        dir_norm = res_norm
    else:
        cross = read_scalar(block, 1)
        beta = res_norm / (sc_prev[0:1, 0:1] + NORM_GUARD)
        s = u + beta * s_prev[...]
        dir_norm = res_norm + 2.0 * beta * cross + beta * beta * sc_prev[1:2, 0:1]
    prob = p_ref[...]
    mixed = jnp.sum(prob * s, axis=0, keepdims=True)
    c = (scale_ref[...] * prob * (s - mixed)).astype(BF16)
    curv = sum_all(s * c.astype(F32))
    return s, c, curv, res_norm, dir_norm, beta


def curv_kernel(*refs, n, first):
    parts, refs = refs[:n], refs[n:]
    s_prev, sc_prev = None, None
    if not first:
        (s_prev, sc_prev), refs = refs[:2], refs[2:]
    p_ref, scale_ref, x_ref, s_ref, c_ref, send_ref, block_ref, sc_ref = refs
    s, c, curv, res_norm, dir_norm, beta = curvature(parts, s_prev, sc_prev, p_ref, scale_ref)
    s_ref[...] = s
    c_ref[...] = c
    sc_ref[0:1, :] = jnp.broadcast_to(res_norm, (1, LANES))
    sc_ref[1:2, :] = jnp.broadcast_to(dir_norm, (1, LANES))
    sc_ref[2:3, :] = jnp.broadcast_to(beta, (1, LANES))
    sc_ref[3:, :] = jnp.zeros((5, LANES), F32)
    block = scalar_block((curv,), lax.axis_index("dp"))
    half = x_ref.shape[1] // 2
    block_ref[...] = block
    send_ref[:, half:] = block.astype(BF16)
    column_half(c, x_ref, 1 - my_core(), send_ref)


def own_columns_kernel(c_ref, block_ref, x_ref, out_ref):
    half = x_ref.shape[1] // 2
    out_ref[:, half:] = block_ref[...]
    column_half(c_ref[...], x_ref, my_core(), out_ref)


def residual_out(residual, extra, r_ref, send_ref):
    half = residual.shape[1]
    r_ref[...] = residual
    send_ref[:, :half] = residual.astype(BF16)
    send_ref[:, half:] = scalar_block((sum_all(residual * residual),) + extra, 0).astype(BF16)


def gradient_kernel(*refs, n):
    parts, (w_ref, weight_ref, r_ref, send_ref, scale_ref, loss_ref) = refs[:n], refs[n:]
    total = add_up(parts)
    half = r_ref.shape[1]
    block = total[:, half:]
    weight_total = read_scalar(block, 0)
    loss_ref[...] = jnp.broadcast_to(read_scalar(block, 1) / weight_total, loss_ref.shape)
    scale_ref[...] = weight_ref[...].astype(F32) / weight_total
    weight = w_ref[:, pl.ds(pl.multiple_of(my_core() * half, LANES), half)]
    residual = -(total[:, :half] / weight_total + RIDGE_COEF * weight)
    residual_out(residual, (), r_ref, send_ref)


def update_kernel(*refs, n, first):
    parts, refs = refs[:n], refs[n:]
    (r_ref, sc_ref), refs = refs[:2], refs[2:]
    if first:
        r_out, d_out, send_ref, alpha_ref = refs
        direction = r_ref[...]
    else:
        d_ref, r_out, d_out, send_ref, alpha_ref = refs
        direction = r_ref[...] + sc_ref[2:3, 0:1] * d_ref[...]
    total = add_up(parts)
    half = r_ref.shape[1]
    curv = read_scalar(total[:, half:], 0) + RIDGE_COEF * sc_ref[1:2, 0:1]
    alpha = sc_ref[0:1, 0:1] / curv
    residual = r_ref[...] - alpha * (total[:, :half] + RIDGE_COEF * direction)
    d_out[...] = direction
    alpha_ref[...] = jnp.broadcast_to(alpha, alpha_ref.shape)
    residual_out(residual, (sum_all(residual * direction),), r_out, send_ref)


def row_half(h, x_ref, which, step, i):
    half = x_ref.shape[1] // 2
    cols = half_columns(x_ref, which, half, 0)
    return lax.dot_general(
        h, x_ref[i * step : (i + 1) * step, cols], NT, preferred_element_type=F32
    )


def own_rows_kernel(send_ref, x_ref, out_ref, *, step):
    half = x_ref.shape[1] // 2
    h = send_ref[:, :half]
    for i in range(x_ref.shape[0] // step):
        out_ref[:, i * step : (i + 1) * step] = row_half(h, x_ref, my_core(), step, i)


def mate_rows_kernel(acc_ref, mine_ref, recv_ref, x_ref, out_ref, *, step):
    half = x_ref.shape[1] // 2
    rows = x_ref.shape[0]
    h = recv_ref[:, :half]
    block = mine_ref[:, half:].astype(F32) + recv_ref[:, half:].astype(F32)
    lane = lax.axis_index("feat")
    out_ref[:, rows:] = scalar_block((read_scalar(block, 0), read_scalar(block, 1)), lane).astype(
        BF16
    )
    for i in range(rows // step):
        cols = slice(i * step, (i + 1) * step)
        out_ref[:, cols] = (acc_ref[:, cols] + row_half(h, x_ref, 1 - my_core(), step, i)).astype(
            BF16
        )


def last_kernel(*refs, n):
    parts, (s_prev, sc_prev, p_ref, scale_ref, s_ref, curv_ref) = refs[:n], refs[n:]
    s, c, curv, res_norm, dir_norm, beta = curvature(parts, s_prev, sc_prev, p_ref, scale_ref)
    s_ref[...] = s
    curv_ref[0:1, :] = jnp.broadcast_to(curv, (1, LANES))
    curv_ref[1:2, :] = jnp.broadcast_to(dir_norm, (1, LANES))
    curv_ref[2:3, :] = jnp.broadcast_to(res_norm, (1, LANES))
    curv_ref[3:, :] = jnp.zeros((5, LANES), F32)


def call(kernel, name, outs, *args, scratch=(), keep=()):
    specs = [
        pl.BlockSpec(memory_space=pl.ANY if i in keep else pltpu.VMEM) for i in range(len(args))
    ]
    return pl.pallas_call(
        kernel,
        out_shape=tuple(pltpu.VMEM(shape, dtype) for shape, dtype in outs),
        in_specs=specs,
        out_specs=tuple(pl.BlockSpec(memory_space=pltpu.VMEM) for _ in outs),
        scratch_shapes=scratch,
        compiler_params=pltpu.CompilerParams(vmem_limit_bytes=VMEM_LIMIT),
        name=name,
    )(*args)


def swap(value, axis, size, bit):
    return lax.ppermute(value, axis, [(i, i ^ bit) for i in range(size)])


def gather_sum(value, axis, size, bits):
    kind = value.dtype
    while len(bits) > 2:
        value = (value.astype(F32) + swap(value, axis, size, bits[0]).astype(F32)).astype(kind)
        bits = bits[1:]
    if len(bits) == 1:
        return [value, swap(value, axis, size, bits[0])]
    a, b = bits
    return [value] + [swap(value, axis, size, k) for k in (a, b, a | b)]


def bits_of(size):
    return [1 << i for i in range(size.bit_length() - 1)]


def on_device(features, weight, labels, sample_weight, *, dp, feat):
    classes, columns = weight.shape
    rows = features.shape[0]
    half = columns // 2
    labels = labels.reshape(1, rows)
    row_weight = sample_weight.reshape(1, rows)
    across_feat = functools.partial(gather_sum, axis="feat", size=feat, bits=bits_of(feat))
    across_chips = functools.partial(gather_sum, axis="dp", size=dp, bits=bits_of(dp)[1:])

    def core_swap(value):
        return swap(value, "dp", dp, 1)

    chunks = 12
    x, logit_part = call(
        functools.partial(load_kernel, chunks=chunks, ahead=3),
        "load",
        [((rows, columns), BF16), ((classes, rows), F32)],
        features,
        weight,
        scratch=(pltpu.SemaphoreType.DMA((chunks,)),),
        keep=(0,),
    )
    x = pltpu.with_memory_space_constraint(x, pltpu.VMEM)

    def column_sums(c, send, block):
        received = core_swap(send)
        (own,) = call(
            own_columns_kernel, "own_columns", [((classes, half + LANES), F32)], c, block, x
        )
        return across_chips((own + received.astype(F32)).astype(BF16))

    def row_sums(send):
        received = core_swap(send)
        (part,) = call(
            functools.partial(own_rows_kernel, step=256),
            "own_rows",
            [((classes, rows), F32)],
            send,
            x,
        )
        (score,) = call(
            functools.partial(mate_rows_kernel, step=256),
            "mate_rows",
            [((classes, rows + LANES), BF16)],
            part,
            send,
            received,
            x,
        )
        return across_feat(score)

    curv_outs = [
        ((classes, rows), BF16),
        ((classes, half + LANES), BF16),
        ((16, LANES), F32),
    ]
    parts = across_feat(logit_part)
    prob, e, send, block = call(
        functools.partial(probs_kernel, n=len(parts)),
        "probs",
        [((classes, rows), F32)] + curv_outs,
        *parts,
        labels,
        row_weight,
        x,
    )
    parts = column_sums(e, send, block)
    residual, send, scale, loss = call(
        functools.partial(gradient_kernel, n=len(parts)),
        "gradient",
        [((classes, half), F32), ((classes, half + LANES), BF16), ((1, rows), F32), ((8, LANES), F32)],
        *parts,
        weight,
        row_weight,
    )
    state, steps, scores = (), [], []
    direction = ()
    for i in range(CG_ITERS - 1):
        parts = row_sums(send)
        s, c, send, block, sc = call(
            functools.partial(curv_kernel, n=len(parts), first=i == 0),
            "curvature",
            [((classes, rows), F32)] + curv_outs + [((8, LANES), F32)],
            *parts,
            *state,
            prob,
            scale,
            x,
        )
        state = (s, sc)
        scores.append(s)
        parts = column_sums(c, send, block)
        residual, new_direction, send, alpha = call(
            functools.partial(update_kernel, n=len(parts), first=i == 0),
            "update",
            [((classes, half), F32)] * 2 + [((classes, half + LANES), BF16), ((8, LANES), F32)],
            *parts,
            residual,
            sc,
            *direction,
        )
        direction = (new_direction,)
        steps.append(alpha)
    parts = row_sums(send)
    s, sc = call(
        functools.partial(last_kernel, n=len(parts)),
        "last",
        [((classes, rows), F32), ((8, LANES), F32)],
        *parts,
        *state,
        prob,
        scale,
    )
    scores.append(s)
    curv = sc[0:1]
    for bit in bits_of(dp):
        curv = curv + swap(curv, "dp", dp, bit)
    last = sc[2:3] / (curv + RIDGE_COEF * sc[1:2])
    steps.append(last)
    total = sum(a[0, 0] * s for a, s in zip(steps, scores))
    return total.T, loss[0, 0]


def solution(mesh):
    dp, feat = mesh.shape["dp"], mesh.shape["feat"]
    in_specs = (P("dp", "feat"), P(None, "feat"), P("dp"), P("dp"))
    out_specs = (P("dp", None), P())
    return jax.shard_map(
        functools.partial(on_device, dp=dp, feat=feat),
        mesh=mesh,
        in_specs=in_specs,
        out_specs=out_specs,
        check_vma=False,
    )
```

```python
import functools
import math

import jax
import jax.numpy as jnp
from jax import lax
from jax.sharding import PartitionSpec as P
import jax.experimental.pallas as pl
import jax.experimental.pallas.tpu as pltpu

CG_ITERS = 4
RIDGE_COEF = 0.1
NORM_GUARD = 1e-06
LANES = 128
VMEM_LIMIT = 4 * 2**20
TURNED = 3

F32 = jnp.float32
BF16 = jnp.bfloat16
NT = (((1,), (1,)), ((), ()))
NN = (((1,), (0,)), ((), ()))


def scalar_block(values, lane):
    rows = lax.broadcasted_iota(jnp.int32, (16, LANES), 0)
    lanes = lax.broadcasted_iota(jnp.int32, (16, LANES), 1)
    block = jnp.zeros((16, LANES), F32)
    for i, value in enumerate(values):
        rest = jnp.broadcast_to(value, (16, LANES))
        for part in range(3):
            piece = rest.astype(BF16).astype(F32)
            block = jnp.where(rows == 3 * i + part, piece, block)
            rest = rest - piece
    return jnp.where(lanes == lane, block, 0.0)


def read_scalar(block, i):
    rows = lax.broadcasted_iota(jnp.int32, (16, LANES), 0)
    mine = (rows >= 3 * i) & (rows < 3 * i + 3)
    return jnp.sum(jnp.where(mine, block, 0.0), keepdims=True)


def sum_all(value):
    return jnp.sum(value, keepdims=True)


def one_row(ref):
    return jnp.concatenate([ref[i : i + 1, :] for i in range(ref.shape[0])], axis=1)


def add_up(parts):
    values = [p[...].astype(F32) for p in parts]
    while len(values) > 1:
        values = [a + b for a, b in zip(values[::2], values[1::2])]
    return values[0]


def my_core():
    return lax.rem(lax.axis_index("dp"), 2)


class Store:
    def __init__(self, rows, columns):
        self.rows, self.columns = rows, columns
        self.width = math.gcd(math.gcd(rows, columns // 2), 512)
        self.groups = min(TURNED, rows // self.width)
        self.shape = (rows * columns // self.width + self.groups * columns, self.width)

    def block(self, j):
        return pl.ds(pl.multiple_of(j * self.rows, self.width), self.rows)

    def turned(self, i, first, count):
        start = self.rows * self.columns // self.width + i * self.columns + first
        return pl.ds(pl.multiple_of(start, LANES), count)


def load_kernel(x_hbm, w_hbm, x_ref, w_ref, l_ref, sems, w_sem, *, store, ahead):
    width = store.width
    blocks = store.columns // width

    def copy(j):
        cols = pl.ds(pl.multiple_of(j * width, width), width)
        return pltpu.make_async_copy(x_hbm.at[:, cols], x_ref.at[store.block(j)], sems.at[j])

    w_copy = pltpu.make_async_copy(w_hbm, w_ref, w_sem)
    w_copy.start()
    for j in range(min(ahead, blocks)):
        copy(j).start()
    l_ref[...] = jnp.zeros(l_ref.shape, F32)
    w_copy.wait()

    @pl.loop(0, blocks)
    def _(j):
        copy(j).wait()

        @pl.when(j + ahead < blocks)
        def _():
            copy(j + ahead).start()

        first = pl.multiple_of(j * width, width)
        w = w_ref[:, pl.ds(first, width)].astype(BF16)
        for i in range(store.rows // width):
            rows = pl.ds(pl.multiple_of(j * store.rows + i * width, width), width)
            turned = x_ref[rows, :].T
            if i < store.groups:
                x_ref[store.turned(i, first, width), :] = turned
            l_ref[:, i * width : (i + 1) * width] += lax.dot_general(
                w, turned, NN, preferred_element_type=F32
            )


def column_half(c, x_ref, which, out_ref, store):
    width = store.width
    count = store.columns // 2 // width
    for i in range(count):
        block = lax.dot_general(
            c, x_ref[store.block(which * count + i), :], NN, preferred_element_type=F32
        )
        out_ref[:, i * width : (i + 1) * width] = block.astype(out_ref.dtype)


def probs_kernel(*refs, n, store):
    parts, (labels_ref, weight_ref, x_ref, p_ref, e_ref, send_ref, block_ref) = refs[:n], refs[n:]
    logits = add_up(parts)
    classes = logits.shape[0]
    top = jnp.max(logits, axis=0, keepdims=True)
    shifted = jnp.exp(logits - top)
    summed = jnp.sum(shifted, axis=0, keepdims=True)
    prob = shifted / summed
    log_total = top + jnp.log(summed)
    row_weight = one_row(weight_ref).astype(F32)
    rows = lax.broadcasted_iota(jnp.int32, logits.shape, 0)
    onehot = (rows == one_row(labels_ref)).astype(F32)
    picked = jnp.sum(logits * onehot, axis=0, keepdims=True)
    p_ref[...] = prob
    e = (row_weight * (prob - onehot)).astype(BF16)
    e_ref[...] = e
    block = scalar_block(
        (sum_all(row_weight), sum_all(row_weight * (log_total - picked))), lax.axis_index("dp")
    )
    half = store.columns // 2
    block_ref[...] = block
    send_ref[:, half:] = block.astype(BF16)
    column_half(e, x_ref, 1 - my_core(), send_ref, store)


def curvature(parts, s_prev, sc_prev, p_ref, scale_ref):
    total = add_up(parts)
    rows = p_ref.shape[1]
    block = total[:, rows:]
    u = total[:, :rows]
    res_norm = read_scalar(block, 0)
    if s_prev is None:
        beta = jnp.zeros((1, 1), F32)
        s = u
        dir_norm = res_norm
    else:
        cross = read_scalar(block, 1)
        beta = res_norm / (sc_prev[0:1, 0:1] + NORM_GUARD)
        s = u + beta * s_prev[...]
        dir_norm = res_norm + 2.0 * beta * cross + beta * beta * sc_prev[1:2, 0:1]
    prob = p_ref[...]
    mixed = jnp.sum(prob * s, axis=0, keepdims=True)
    c = (scale_ref[...] * prob * (s - mixed)).astype(BF16)
    curv = sum_all(s * c.astype(F32))
    return s, c, curv, res_norm, dir_norm, beta


def curv_kernel(*refs, n, first, store):
    parts, refs = refs[:n], refs[n:]
    s_prev, sc_prev = None, None
    if not first:
        (s_prev, sc_prev), refs = refs[:2], refs[2:]
    p_ref, scale_ref, x_ref, s_ref, c_ref, send_ref, block_ref, sc_ref = refs
    s, c, curv, res_norm, dir_norm, beta = curvature(parts, s_prev, sc_prev, p_ref, scale_ref)
    s_ref[...] = s
    c_ref[...] = c
    sc_ref[0:1, :] = jnp.broadcast_to(res_norm, (1, LANES))
    sc_ref[1:2, :] = jnp.broadcast_to(dir_norm, (1, LANES))
    sc_ref[2:3, :] = jnp.broadcast_to(beta, (1, LANES))
    sc_ref[3:, :] = jnp.zeros((5, LANES), F32)
    block = scalar_block((curv,), lax.axis_index("dp"))
    half = store.columns // 2
    block_ref[...] = block
    send_ref[:, half:] = block.astype(BF16)
    column_half(c, x_ref, 1 - my_core(), send_ref, store)


def own_columns_kernel(c_ref, block_ref, x_ref, out_ref, *, store):
    half = store.columns // 2
    out_ref[:, half:] = block_ref[...]
    column_half(c_ref[...], x_ref, my_core(), out_ref, store)


def residual_out(residual, extra, r_ref, send_ref):
    half = residual.shape[1]
    r_ref[...] = residual
    send_ref[:, :half] = residual.astype(BF16)
    send_ref[:, half:] = scalar_block((sum_all(residual * residual),) + extra, 0).astype(BF16)


def gradient_kernel(*refs, n):
    parts, (w_ref, weight_ref, r_ref, send_ref, scale_ref, loss_ref) = refs[:n], refs[n:]
    total = add_up(parts)
    half = r_ref.shape[1]
    block = total[:, half:]
    weight_total = read_scalar(block, 0)
    loss_ref[...] = jnp.broadcast_to(read_scalar(block, 1) / weight_total, loss_ref.shape)
    scale_ref[...] = one_row(weight_ref).astype(F32) / weight_total
    weight = w_ref[:, pl.ds(pl.multiple_of(my_core() * half, LANES), half)]
    residual = -(total[:, :half] / weight_total + RIDGE_COEF * weight)
    residual_out(residual, (), r_ref, send_ref)


def update_kernel(*refs, n, first):
    parts, refs = refs[:n], refs[n:]
    (r_ref, sc_ref), refs = refs[:2], refs[2:]
    if first:
        r_out, d_out, send_ref, alpha_ref = refs
        direction = r_ref[...]
    else:
        d_ref, r_out, d_out, send_ref, alpha_ref = refs
        direction = r_ref[...] + sc_ref[2:3, 0:1] * d_ref[...]
    total = add_up(parts)
    half = r_ref.shape[1]
    curv = read_scalar(total[:, half:], 0) + RIDGE_COEF * sc_ref[1:2, 0:1]
    alpha = sc_ref[0:1, 0:1] / curv
    residual = r_ref[...] - alpha * (total[:, :half] + RIDGE_COEF * direction)
    d_out[...] = direction
    alpha_ref[...] = jnp.broadcast_to(alpha, alpha_ref.shape)
    residual_out(residual, (sum_all(residual * direction),), r_out, send_ref)


def row_half(h, x_ref, which, store, i):
    half, width = store.columns // 2, store.width
    if i < store.groups:
        return lax.dot_general(
            h, x_ref[store.turned(i, which * half, half), :], NN, preferred_element_type=F32
        )
    total = jnp.zeros((h.shape[0], width), F32)
    for j in range(half // width):
        first = (which * (half // width) + j) * store.rows + i * width
        block = x_ref[pl.ds(pl.multiple_of(first, width), width), :]
        total += lax.dot_general(
            h[:, j * width : (j + 1) * width], block, NT, preferred_element_type=F32
        )
    return total


def own_rows_kernel(send_ref, x_ref, out_ref, *, store):
    half, width = store.columns // 2, store.width
    h = send_ref[:, :half]
    for i in range(store.rows // width):
        out_ref[:, i * width : (i + 1) * width] = row_half(h, x_ref, my_core(), store, i)


def mate_rows_kernel(acc_ref, mine_ref, recv_ref, x_ref, out_ref, *, store):
    half, width = store.columns // 2, store.width
    h = recv_ref[:, :half]
    block = mine_ref[:, half:].astype(F32) + recv_ref[:, half:].astype(F32)
    lane = lax.axis_index("feat")
    out_ref[:, store.rows :] = scalar_block(
        (read_scalar(block, 0), read_scalar(block, 1)), lane
    ).astype(BF16)
    for i in range(store.rows // width):
        cols = slice(i * width, (i + 1) * width)
        part = acc_ref[:, cols] + row_half(h, x_ref, 1 - my_core(), store, i)
        out_ref[:, cols] = part.astype(BF16)


def last_kernel(*refs, n):
    parts, (s_prev, sc_prev, p_ref, scale_ref, s_ref, curv_ref) = refs[:n], refs[n:]
    s, c, curv, res_norm, dir_norm, beta = curvature(parts, s_prev, sc_prev, p_ref, scale_ref)
    s_ref[...] = s
    curv_ref[0:1, :] = jnp.broadcast_to(curv, (1, LANES))
    curv_ref[1:2, :] = jnp.broadcast_to(dir_norm, (1, LANES))
    curv_ref[2:3, :] = jnp.broadcast_to(res_norm, (1, LANES))
    curv_ref[3:, :] = jnp.zeros((5, LANES), F32)


def finish_kernel(curv_ref, sc_ref, loss_ref, *refs):
    count = (len(refs) - 2) // 2
    steps, scores, (out_ref, loss_out) = refs[:count], refs[count:-2], refs[-2:]
    loss_out[0, 0] = jnp.max(loss_ref[...])
    last = sc_ref[2:3, 0:1] / (curv_ref[0:1, 0:1] + RIDGE_COEF * sc_ref[1:2, 0:1])
    total = last * scores[-1][...]
    for alpha, score in zip(steps, scores[:-1]):
        total += alpha[0:1, 0:1] * score[...]
    out_ref[...] = total


def add_kernel(*refs):
    refs[-1][...] = add_up(refs[:-1]).astype(refs[-1].dtype)


def call(kernel, name, outs, *args, pins=(), scratch=(), keep=(), out_space=pltpu.VMEM, out_specs=(), limit=VMEM_LIMIT):
    def body(*refs):
        kernel(*refs[: len(args)], *refs[len(args) + len(pins) :])

    args_pins = args + tuple(pltpu.with_memory_space_constraint(p, pltpu.VMEM) for p in pins)
    specs = [
        pl.BlockSpec(memory_space=pl.ANY if i in keep else pltpu.VMEM)
        for i in range(len(args_pins))
    ]
    return pl.pallas_call(
        body,
        out_shape=tuple(out_space(shape, dtype) for shape, dtype in outs),
        in_specs=specs,
        out_specs=tuple(pl.BlockSpec(memory_space=m) for m in out_specs or [pltpu.VMEM] * len(outs)),
        scratch_shapes=scratch,
        compiler_params=pltpu.CompilerParams(vmem_limit_bytes=limit),
        name=name,
    )(*args_pins)


def add(pins, *values, kind):
    return call(add_kernel, "add", [(values[0].shape, kind)], *values, pins=pins)[0]


def swap(value, axis, size, bit):
    return lax.ppermute(value, axis, [(i, i ^ bit) for i in range(size)])


def gather_sum(value, pins, axis, size, bits):
    kind = value.dtype
    while len(bits) > 2:
        value = add(pins, value, swap(value, axis, size, bits[0]), kind=kind)
        bits = bits[1:]
    if len(bits) == 1:
        return [value, swap(value, axis, size, bits[0])]
    a, b = bits
    return [value] + [swap(value, axis, size, k) for k in (a, b, a | b)]


def bits_of(size):
    return [1 << i for i in range(size.bit_length() - 1)]


def on_device(features, weight, labels, sample_weight, *, dp, feat):
    classes, columns = weight.shape
    rows = features.shape[0]
    half = columns // 2
    labels = labels.reshape(rows // LANES, LANES)
    row_weight = sample_weight.reshape(rows // LANES, LANES)
    across_feat = functools.partial(gather_sum, axis="feat", size=feat, bits=bits_of(feat))
    across_chips = functools.partial(gather_sum, axis="dp", size=dp, bits=bits_of(dp)[1:])

    def core_swap(value):
        return swap(value, "dp", dp, 1)

    store = Store(rows, columns)
    x, weight, logit_part = call(
        functools.partial(load_kernel, store=store, ahead=4),
        "load",
        [(store.shape, BF16), ((classes, columns), F32), ((classes, rows), F32)],
        features,
        weight,
        scratch=(pltpu.SemaphoreType.DMA((columns // store.width,)), pltpu.SemaphoreType.DMA),
        keep=(0, 1),
        limit=VMEM_LIMIT - weight.size * weight.dtype.itemsize,
    )
    x = pltpu.with_memory_space_constraint(x, pltpu.VMEM)
    pins = [x, weight]

    def column_sums(c, send, block):
        received = core_swap(send)
        (own,) = call(
            functools.partial(own_columns_kernel, store=store),
            "own_columns",
            [((classes, half + LANES), F32)],
            c,
            block,
            x,
            pins=pins,
        )
        return across_chips(add(pins, own, received, kind=BF16), pins)

    def row_sums(send):
        received = core_swap(send)
        (part,) = call(
            functools.partial(own_rows_kernel, store=store),
            "own_rows",
            [((classes, rows), F32)],
            send,
            x,
            pins=pins,
        )
        (score,) = call(
            functools.partial(mate_rows_kernel, store=store),
            "mate_rows",
            [((classes, rows + LANES), BF16)],
            part,
            send,
            received,
            x,
            pins=pins,
        )
        return across_feat(score, pins)

    curv_outs = [
        ((classes, rows), BF16),
        ((classes, half + LANES), BF16),
        ((16, LANES), F32),
    ]
    parts = across_feat(logit_part, pins)
    prob, e, send, block = call(
        functools.partial(probs_kernel, n=len(parts), store=store),
        "probs",
        [((classes, rows), F32)] + curv_outs,
        *parts,
        labels,
        row_weight,
        x,
        pins=pins,
    )
    parts = column_sums(e, send, block)
    residual, send, scale, loss = call(
        functools.partial(gradient_kernel, n=len(parts)),
        "gradient",
        [((classes, half), F32), ((classes, half + LANES), BF16), ((1, rows), F32), ((8, LANES), F32)],
        *parts,
        weight,
        row_weight,
        pins=pins,
    )
    pins[1:] = [residual]
    state, steps, scores = (), [], []
    direction = ()
    for i in range(CG_ITERS - 1):
        parts = row_sums(send)
        s, c, send, block, sc = call(
            functools.partial(curv_kernel, n=len(parts), first=i == 0, store=store),
            "curvature",
            [((classes, rows), F32)] + curv_outs + [((8, LANES), F32)],
            *parts,
            *state,
            prob,
            scale,
            x,
            pins=pins,
        )
        state = (s, sc)
        scores.append(s)
        parts = column_sums(c, send, block)
        residual, new_direction, send, alpha = call(
            functools.partial(update_kernel, n=len(parts), first=i == 0),
            "update",
            [((classes, half), F32)] * 2 + [((classes, half + LANES), BF16), ((8, LANES), F32)],
            *parts,
            residual,
            sc,
            *direction,
            pins=pins,
        )
        pins[1:] = [residual, new_direction] if i < CG_ITERS - 2 else []
        direction = (new_direction,)
        steps.append(alpha)
    parts = row_sums(send)
    s, sc = call(
        functools.partial(last_kernel, n=len(parts)),
        "last",
        [((classes, rows), F32), ((8, LANES), F32)],
        *parts,
        *state,
        prob,
        scale,
        pins=pins,
    )
    scores.append(s)
    curv = sc
    for bit in bits_of(dp):
        curv = add(pins, curv, swap(curv, "dp", dp, bit), kind=F32)
    out, loss = call(
        finish_kernel,
        "finish",
        [((classes, rows), F32), ((1, 1), F32)],
        curv,
        sc,
        loss,
        *steps,
        *scores,
        out_space=jax.ShapeDtypeStruct,
        out_specs=(pltpu.VMEM, pltpu.SMEM),
    )
    return out.T, loss.reshape(())


def solution(mesh):
    dp, feat = mesh.shape["dp"], mesh.shape["feat"]
    in_specs = (P("dp", "feat"), P(None, "feat"), P("dp"), P("dp"))
    out_specs = (P("dp", None), P())
    return jax.shard_map(
        functools.partial(on_device, dp=dp, feat=feat),
        mesh=mesh,
        in_specs=in_specs,
        out_specs=out_specs,
        check_vma=False,
    )
```

```python
import functools
import math

import jax
import jax.numpy as jnp
from jax import lax
from jax.sharding import PartitionSpec as P
import jax.experimental.pallas as pl
import jax.experimental.pallas.tpu as pltpu

CG_ITERS = 4
RIDGE_COEF = 0.1
NORM_GUARD = 1e-06
LANES = 128
VMEM_LIMIT = 4 * 2**20
TURNED = 3

F32 = jnp.float32
BF16 = jnp.bfloat16
NT = (((1,), (1,)), ((), ()))
NN = (((1,), (0,)), ((), ()))


def scalar_block(values, lane):
    rows = lax.broadcasted_iota(jnp.int32, (16, LANES), 0)
    lanes = lax.broadcasted_iota(jnp.int32, (16, LANES), 1)
    block = jnp.zeros((16, LANES), F32)
    for i, value in enumerate(values):
        rest = jnp.broadcast_to(value, (16, LANES))
        for part in range(3):
            piece = rest.astype(BF16).astype(F32)
            block = jnp.where(rows == 3 * i + part, piece, block)
            rest = rest - piece
    return jnp.where(lanes == lane, block, 0.0)


def read_scalar(block, i):
    rows = lax.broadcasted_iota(jnp.int32, (16, LANES), 0)
    mine = (rows >= 3 * i) & (rows < 3 * i + 3)
    return jnp.sum(jnp.where(mine, block, 0.0), keepdims=True)


def sum_all(value):
    return jnp.sum(value, keepdims=True)


def one_row(ref):
    return jnp.concatenate([ref[i : i + 1, :] for i in range(ref.shape[0])], axis=1)


def add_up(parts):
    values = [p[...].astype(F32) for p in parts]
    while len(values) > 1:
        values = [a + b for a, b in zip(values[::2], values[1::2])]
    return values[0]


def my_core():
    return lax.rem(lax.axis_index("dp"), 2)


def half_of(which, half):
    return pl.ds(pl.multiple_of(which * half, LANES), half)


def load_kernel(x_hbm, w_hbm, x_ref, xt_ref, w_ref, l_ref, sems, w_sem, *, step, ahead):
    rows, columns = x_ref.shape
    chunks = rows // step
    block = math.gcd(columns, 512)

    def rows_of(i):
        return pl.ds(pl.multiple_of(i * step, step), step)

    def copy(i):
        return pltpu.make_async_copy(x_hbm.at[rows_of(i)], x_ref.at[rows_of(i)], sems.at[i])

    w_copy = pltpu.make_async_copy(w_hbm, w_ref, w_sem)
    w_copy.start()
    for i in range(min(ahead, chunks)):
        copy(i).start()
    w_copy.wait()

    @pl.loop(0, chunks)
    def _(i):
        copy(i).wait()

        @pl.when(i + ahead < chunks)
        def _():
            copy(i + ahead).start()

        total = jnp.zeros((w_ref.shape[0], step), F32)
        for j in range(0, columns, block):
            turned = x_ref[rows_of(i), j : j + block].T
            xt_ref[j : j + block, rows_of(i)] = turned
            w = w_ref[:, j : j + block].astype(BF16)
            total += lax.dot_general(w, turned, NN, preferred_element_type=F32)
        l_ref[:, rows_of(i)] = total


def column_half(c, x_ref, which, out_ref):
    half = x_ref.shape[1] // 2
    width = math.gcd(half, 512)
    for i in range(0, half, width):
        cols = pl.ds(pl.multiple_of(which * half + i, width), width)
        block = lax.dot_general(c, x_ref[:, cols], NN, preferred_element_type=F32)
        out_ref[:, i : i + width] = block.astype(out_ref.dtype)


def probs_kernel(*refs, n):
    parts, (labels_ref, weight_ref, x_ref, p_ref, e_ref, send_ref, block_ref) = refs[:n], refs[n:]
    logits = add_up(parts)
    classes = logits.shape[0]
    top = jnp.max(logits, axis=0, keepdims=True)
    shifted = jnp.exp(logits - top)
    summed = jnp.sum(shifted, axis=0, keepdims=True)
    prob = shifted / summed
    log_total = top + jnp.log(summed)
    row_weight = one_row(weight_ref).astype(F32)
    rows = lax.broadcasted_iota(jnp.int32, logits.shape, 0)
    onehot = (rows == one_row(labels_ref)).astype(F32)
    picked = jnp.sum(logits * onehot, axis=0, keepdims=True)
    p_ref[...] = prob
    e = (row_weight * (prob - onehot)).astype(BF16)
    e_ref[...] = e
    block = scalar_block(
        (sum_all(row_weight), sum_all(row_weight * (log_total - picked))), lax.axis_index("dp")
    )
    half = x_ref.shape[1] // 2
    block_ref[...] = block
    send_ref[:, half:] = block.astype(BF16)
    column_half(e, x_ref, 1 - my_core(), send_ref)


def curvature(parts, s_prev, sc_prev, p_ref, scale_ref):
    total = add_up(parts)
    rows = p_ref.shape[1]
    block = total[:, rows:]
    u = total[:, :rows]
    res_norm = read_scalar(block, 0)
    if s_prev is None:
        beta = jnp.zeros((1, 1), F32)
        s = u
        dir_norm = res_norm
    else:
        cross = read_scalar(block, 1)
        beta = res_norm / (sc_prev[0:1, 0:1] + NORM_GUARD)
        s = u + beta * s_prev[...]
        dir_norm = res_norm + 2.0 * beta * cross + beta * beta * sc_prev[1:2, 0:1]
    prob = p_ref[...]
    mixed = jnp.sum(prob * s, axis=0, keepdims=True)
    c = (scale_ref[...] * prob * (s - mixed)).astype(BF16)
    curv = sum_all(s * c.astype(F32))
    return s, c, curv, res_norm, dir_norm, beta


def curv_kernel(*refs, n, first):
    parts, refs = refs[:n], refs[n:]
    s_prev, sc_prev = None, None
    if not first:
        (s_prev, sc_prev), refs = refs[:2], refs[2:]
    p_ref, scale_ref, x_ref, s_ref, c_ref, send_ref, block_ref, sc_ref = refs
    s, c, curv, res_norm, dir_norm, beta = curvature(parts, s_prev, sc_prev, p_ref, scale_ref)
    s_ref[...] = s
    c_ref[...] = c
    sc_ref[0:1, :] = jnp.broadcast_to(res_norm, (1, LANES))
    sc_ref[1:2, :] = jnp.broadcast_to(dir_norm, (1, LANES))
    sc_ref[2:3, :] = jnp.broadcast_to(beta, (1, LANES))
    sc_ref[3:, :] = jnp.zeros((5, LANES), F32)
    block = scalar_block((curv,), lax.axis_index("dp"))
    half = x_ref.shape[1] // 2
    block_ref[...] = block
    send_ref[:, half:] = block.astype(BF16)
    column_half(c, x_ref, 1 - my_core(), send_ref)


def own_columns_kernel(c_ref, block_ref, x_ref, out_ref):
    half = x_ref.shape[1] // 2
    out_ref[:, half:] = block_ref[...]
    column_half(c_ref[...], x_ref, my_core(), out_ref)


def residual_out(residual, extra, send_ref):
    half = residual.shape[1]
    send_ref[:, :half] = residual.astype(BF16)
    send_ref[:, half:] = scalar_block((sum_all(residual * residual),) + extra, 0).astype(BF16)


def gradient_kernel(*refs, n):
    parts, (w_ref, weight_ref, r_ref, send_ref, scale_ref, loss_ref) = refs[:n], refs[n:]
    total = add_up(parts)
    half = r_ref.shape[1]
    block = total[:, half:]
    weight_total = read_scalar(block, 0)
    loss_ref[...] = jnp.broadcast_to(read_scalar(block, 1) / weight_total, loss_ref.shape)
    scale_ref[...] = one_row(weight_ref).astype(F32) / weight_total
    weight = w_ref[:, pl.ds(pl.multiple_of(my_core() * half, LANES), half)]
    residual = -(total[:, :half] / weight_total + RIDGE_COEF * weight)
    r_ref[...] = residual
    residual_out(residual, (), send_ref)


def update_kernel(*refs, n, first, last):
    parts, refs = refs[:n], refs[n:]
    (r_ref, sc_ref), refs = refs[:2], refs[2:]
    direction = r_ref[...]
    if not first:
        direction = direction + sc_ref[2:3, 0:1] * refs[0][...]
        refs = refs[1:]
    send_ref, alpha_ref = refs[:2]
    total = add_up(parts)
    half = r_ref.shape[1]
    curv = read_scalar(total[:, half:], 0) + RIDGE_COEF * sc_ref[1:2, 0:1]
    alpha = sc_ref[0:1, 0:1] / curv
    residual = r_ref[...] - alpha * (total[:, :half] + RIDGE_COEF * direction)
    if not last:
        r_out, d_out = refs[2:]
        r_out[...] = residual
        d_out[...] = direction
    alpha_ref[...] = jnp.broadcast_to(alpha, alpha_ref.shape)
    residual_out(residual, (sum_all(residual * direction),), send_ref)


def row_blocks(xt_ref):
    rows = xt_ref.shape[1]
    width = math.gcd(rows, 512)
    return [slice(i, i + width) for i in range(0, rows, width)]


def row_half(h, xt_ref, which, block):
    half = xt_ref.shape[0] // 2
    return lax.dot_general(
        h, xt_ref[half_of(which, half), block], NN, preferred_element_type=F32
    )


def own_rows_kernel(send_ref, xt_ref, out_ref):
    h = send_ref[:, : xt_ref.shape[0] // 2]
    for block in row_blocks(xt_ref):
        out_ref[:, block] = row_half(h, xt_ref, my_core(), block)


def mate_rows_kernel(acc_ref, mine_ref, recv_ref, xt_ref, out_ref):
    half, rows = xt_ref.shape[0] // 2, xt_ref.shape[1]
    h = recv_ref[:, :half]
    both = mine_ref[:, half:].astype(F32) + recv_ref[:, half:].astype(F32)
    out_ref[:, rows:] = scalar_block(
        (read_scalar(both, 0), read_scalar(both, 1)), lax.axis_index("feat")
    ).astype(BF16)
    for block in row_blocks(xt_ref):
        part = acc_ref[:, block] + row_half(h, xt_ref, 1 - my_core(), block)
        out_ref[:, block] = part.astype(BF16)


def last_kernel(*refs, n):
    parts, (s_prev, sc_prev, p_ref, scale_ref, s_ref, curv_ref) = refs[:n], refs[n:]
    s, c, curv, res_norm, dir_norm, beta = curvature(parts, s_prev, sc_prev, p_ref, scale_ref)
    s_ref[...] = s
    curv_ref[0:1, :] = jnp.broadcast_to(curv, (1, LANES))
    curv_ref[1:2, :] = jnp.broadcast_to(dir_norm, (1, LANES))
    curv_ref[2:3, :] = jnp.broadcast_to(res_norm, (1, LANES))
    curv_ref[3:, :] = jnp.zeros((5, LANES), F32)


def finish_kernel(curv_ref, sc_ref, loss_ref, *refs):
    count = (len(refs) - 2) // 2
    steps, scores, (out_ref, loss_out) = refs[:count], refs[count:-2], refs[-2:]
    loss_out[0, 0] = jnp.max(loss_ref[...])
    last = sc_ref[2:3, 0:1] / (curv_ref[0:1, 0:1] + RIDGE_COEF * sc_ref[1:2, 0:1])
    total = last * scores[-1][...]
    for alpha, score in zip(steps, scores[:-1]):
        total += alpha[0:1, 0:1] * score[...]
    out_ref[...] = total


def add_kernel(*refs):
    refs[-1][...] = add_up(refs[:-1]).astype(refs[-1].dtype)


def call(kernel, name, outs, *args, pins=(), scratch=(), keep=(), out_space=pltpu.VMEM, out_specs=(), limit=VMEM_LIMIT):
    def body(*refs):
        kernel(*refs[: len(args)], *refs[len(args) + len(pins) :])

    args = tuple(
        pltpu.with_memory_space_constraint(a, pltpu.HBM) if i in keep else a
        for i, a in enumerate(args)
    )
    args_pins = args + tuple(pltpu.with_memory_space_constraint(p, pltpu.VMEM) for p in pins)
    specs = [
        pl.BlockSpec(memory_space=pltpu.HBM if i in keep else pltpu.VMEM)
        for i in range(len(args_pins))
    ]
    return pl.pallas_call(
        body,
        out_shape=tuple(out_space(shape, dtype) for shape, dtype in outs),
        in_specs=specs,
        out_specs=tuple(pl.BlockSpec(memory_space=m) for m in out_specs or [pltpu.VMEM] * len(outs)),
        scratch_shapes=scratch,
        compiler_params=pltpu.CompilerParams(vmem_limit_bytes=limit),
        name=name,
    )(*args_pins)


def add(pins, *values, kind):
    return call(add_kernel, "add", [(values[0].shape, kind)], *values, pins=pins)[0]


def swap(value, axis, size, bit):
    return lax.ppermute(value, axis, [(i, i ^ bit) for i in range(size)])


def gather_sum(value, pins, axis, size, bits):
    kind = value.dtype
    while len(bits) > 2:
        value = add(pins, value, swap(value, axis, size, bits[0]), kind=kind)
        bits = bits[1:]
    if len(bits) == 1:
        return [value, swap(value, axis, size, bits[0])]
    a, b = bits
    return [value] + [swap(value, axis, size, k) for k in (a, a | b, b)]


def bits_of(size):
    return [1 << i for i in range(size.bit_length() - 1)]


def on_device(features, weight, labels, sample_weight, *, dp, feat):
    classes, columns = weight.shape
    rows = features.shape[0]
    half = columns // 2
    labels = labels.reshape(rows // LANES, LANES)
    row_weight = sample_weight.reshape(rows // LANES, LANES)
    across_feat = functools.partial(gather_sum, axis="feat", size=feat, bits=bits_of(feat))
    across_chips = functools.partial(gather_sum, axis="dp", size=dp, bits=bits_of(dp)[1:])

    def core_swap(value):
        return swap(value, "dp", dp, 1)

    step = math.gcd(rows, 256)
    x, xt, weight, logit_part = call(
        functools.partial(load_kernel, step=step, ahead=2),
        "load",
        [
            ((rows, columns), BF16),
            ((columns, rows), BF16),
            ((classes, columns), F32),
            ((classes, rows), F32),
        ],
        features,
        weight,
        scratch=(pltpu.SemaphoreType.DMA((rows // step,)), pltpu.SemaphoreType.DMA),
        keep=(0, 1),
        limit=VMEM_LIMIT,
    )
    pins = [x, xt, weight]

    def column_sums(c, send, block):
        received = core_swap(send)
        (own,) = call(
            own_columns_kernel,
            "own_columns",
            [((classes, half + LANES), F32)],
            c,
            block,
            x,
            pins=pins,
        )
        return across_chips(add(pins, own, received, kind=BF16), pins)

    def row_sums(send):
        received = core_swap(send)
        (part,) = call(
            own_rows_kernel,
            "own_rows",
            [((classes, rows), F32)],
            send,
            xt,
            pins=pins,
        )
        (score,) = call(
            mate_rows_kernel,
            "mate_rows",
            [((classes, rows + LANES), BF16)],
            part,
            send,
            received,
            xt,
            pins=pins,
        )
        return across_feat(score, pins)

    curv_outs = [
        ((classes, rows), BF16),
        ((classes, half + LANES), BF16),
        ((16, LANES), F32),
    ]
    parts = across_feat(logit_part, pins)
    prob, e, send, block = call(
        functools.partial(probs_kernel, n=len(parts)),
        "probs",
        [((classes, rows), F32)] + curv_outs,
        *parts,
        labels,
        row_weight,
        x,
        pins=pins,
    )
    parts = column_sums(e, send, block)
    residual, send, scale, loss = call(
        functools.partial(gradient_kernel, n=len(parts)),
        "gradient",
        [((classes, half), F32), ((classes, half + LANES), BF16), ((1, rows), F32), ((8, LANES), F32)],
        *parts,
        weight,
        row_weight,
        pins=pins,
    )
    pins[2:] = [residual]
    state, steps, scores = (), [], []
    direction = ()
    for i in range(CG_ITERS - 1):
        parts = row_sums(send)
        s, c, send, block, sc = call(
            functools.partial(curv_kernel, n=len(parts), first=i == 0),
            "curvature",
            [((classes, rows), F32)] + curv_outs + [((8, LANES), F32)],
            *parts,
            *state,
            prob,
            scale,
            x,
            pins=pins,
        )
        state = (s, sc)
        scores.append(s)
        parts = column_sums(c, send, block)
        last = i == CG_ITERS - 2
        send, alpha, *vectors = call(
            functools.partial(update_kernel, n=len(parts), first=i == 0, last=last),
            "update",
            [((classes, half + LANES), BF16), ((8, LANES), F32)]
            + [((classes, half), F32)] * (0 if last else 2),
            *parts,
            residual,
            sc,
            *direction,
            pins=pins,
        )
        pins[2:] = vectors
        if not last:
            residual, *direction = vectors
        steps.append(alpha)
    parts = row_sums(send)
    s, sc = call(
        functools.partial(last_kernel, n=len(parts)),
        "last",
        [((classes, rows), F32), ((8, LANES), F32)],
        *parts,
        *state,
        prob,
        scale,
        pins=pins,
    )
    scores.append(s)
    curv = sc
    for bit in bits_of(dp):
        curv = add(pins, curv, swap(curv, "dp", dp, bit), kind=F32)
    out, loss = call(
        finish_kernel,
        "finish",
        [((classes, rows), F32), ((1, 1), F32)],
        curv,
        sc,
        loss,
        *steps,
        *scores,
        out_space=jax.ShapeDtypeStruct,
        out_specs=(pltpu.VMEM, pltpu.SMEM),
    )
    return out.T, loss.reshape(())


def solution(mesh):
    dp, feat = mesh.shape["dp"], mesh.shape["feat"]
    in_specs = (P("dp", "feat"), P(None, "feat"), P("dp"), P("dp"))
    out_specs = (P("dp", None), P())
    return jax.shard_map(
        functools.partial(on_device, dp=dp, feat=feat),
        mesh=mesh,
        in_specs=in_specs,
        out_specs=out_specs,
        check_vma=False,
    )
```

```python
import functools
import math

import jax
import jax.numpy as jnp
from jax import lax
from jax.sharding import PartitionSpec as P
import jax.experimental.pallas as pl
import jax.experimental.pallas.tpu as pltpu

CG_ITERS = 4
RIDGE_COEF = 0.1
NORM_GUARD = 1e-06
LANES = 128
VMEM_LIMIT = 4 * 2**20
TURNED = 3

F32 = jnp.float32
BF16 = jnp.bfloat16
NT = (((1,), (1,)), ((), ()))
NN = (((1,), (0,)), ((), ()))


def scalar_block(values, lane):
    rows = lax.broadcasted_iota(jnp.int32, (16, LANES), 0)
    lanes = lax.broadcasted_iota(jnp.int32, (16, LANES), 1)
    block = jnp.zeros((16, LANES), F32)
    for i, value in enumerate(values):
        rest = jnp.broadcast_to(value, (16, LANES))
        for part in range(3):
            piece = rest.astype(BF16).astype(F32)
            block = jnp.where(rows == 3 * i + part, piece, block)
            rest = rest - piece
    return jnp.where(lanes == lane, block, 0.0)


def read_scalar(block, i):
    rows = lax.broadcasted_iota(jnp.int32, (16, LANES), 0)
    mine = (rows >= 3 * i) & (rows < 3 * i + 3)
    return jnp.sum(jnp.where(mine, block, 0.0), keepdims=True)


def sum_all(value):
    return jnp.sum(value, keepdims=True)


def one_row(ref):
    return jnp.concatenate([ref[i : i + 1, :] for i in range(ref.shape[0])], axis=1)


def add_up(parts):
    values = [p[...].astype(F32) for p in parts]
    while len(values) > 1:
        values = [a + b for a, b in zip(values[::2], values[1::2])]
    return values[0]


def my_core():
    return lax.rem(lax.axis_index("dp"), 2)


def load_kernel(x_hbm, w_hbm, x_ref, xt_ref, w_ref, l_ref, sems, w_sem, *, step, ahead):
    rows, columns = x_ref.shape
    chunks = rows // step
    block = math.gcd(columns, 512)

    def rows_of(i):
        return pl.ds(pl.multiple_of(i * step, step), step)

    def copy(i):
        return pltpu.make_async_copy(x_hbm.at[rows_of(i)], x_ref.at[rows_of(i)], sems.at[i])

    w_copy = pltpu.make_async_copy(w_hbm, w_ref, w_sem)
    w_copy.start()
    for i in range(min(ahead, chunks)):
        copy(i).start()
    w_copy.wait()

    @pl.loop(0, chunks)
    def _(i):
        copy(i).wait()

        @pl.when(i + ahead < chunks)
        def _():
            copy(i + ahead).start()

        total = jnp.zeros((w_ref.shape[0], step), F32)
        for j in range(0, columns, block):
            turned = x_ref[rows_of(i), j : j + block].T
            xt_ref[j : j + block, rows_of(i)] = turned
            w = w_ref[:, j : j + block].astype(BF16)
            total += lax.dot_general(w, turned, NN, preferred_element_type=F32)
        l_ref[:, rows_of(i)] = total


def column_part(c, x_ref, which, part, out_ref):
    size = x_ref.shape[1] // 4
    width = math.gcd(size, 512)
    for i in range(0, size, width):
        cols = pl.ds(pl.multiple_of((2 * which + part) * size + i, LANES), width)
        block = lax.dot_general(c, x_ref[:, cols], NN, preferred_element_type=F32)
        out_ref[:, i : i + width] = block.astype(out_ref.dtype)


def send_columns(c, x_ref, block, send0_ref, send1_ref):
    size = x_ref.shape[1] // 4
    send0_ref[:, size:] = block.astype(BF16)
    column_part(c, x_ref, 1 - my_core(), 0, send0_ref)
    column_part(c, x_ref, 1 - my_core(), 1, send1_ref)


def probs_kernel(*refs, n):
    parts, refs = refs[:n], refs[n:]
    labels_ref, weight_ref, x_ref, p_ref, e_ref, send0_ref, send1_ref, block_ref = refs
    logits = add_up(parts)
    classes = logits.shape[0]
    top = jnp.max(logits, axis=0, keepdims=True)
    shifted = jnp.exp(logits - top)
    summed = jnp.sum(shifted, axis=0, keepdims=True)
    prob = shifted / summed
    log_total = top + jnp.log(summed)
    row_weight = one_row(weight_ref).astype(F32)
    rows = lax.broadcasted_iota(jnp.int32, logits.shape, 0)
    onehot = (rows == one_row(labels_ref)).astype(F32)
    picked = jnp.sum(logits * onehot, axis=0, keepdims=True)
    p_ref[...] = prob
    e = (row_weight * (prob - onehot)).astype(BF16)
    e_ref[...] = e
    block = scalar_block(
        (sum_all(row_weight), sum_all(row_weight * (log_total - picked))), lax.axis_index("dp")
    )
    block_ref[...] = block
    send_columns(e, x_ref, block, send0_ref, send1_ref)


def curvature(parts, s_prev, sc_prev, p_ref, scale_ref):
    total = add_up(parts)
    rows = p_ref.shape[1]
    block = total[:, rows:]
    u = total[:, :rows]
    res_norm = read_scalar(block, 0)
    if s_prev is None:
        beta = jnp.zeros((1, 1), F32)
        s = u
        dir_norm = res_norm
    else:
        cross = read_scalar(block, 1)
        beta = res_norm / (sc_prev[0:1, 0:1] + NORM_GUARD)
        s = u + beta * s_prev[...]
        dir_norm = res_norm + 2.0 * beta * cross + beta * beta * sc_prev[1:2, 0:1]
    prob = p_ref[...]
    mixed = jnp.sum(prob * s, axis=0, keepdims=True)
    c = (scale_ref[...] * prob * (s - mixed)).astype(BF16)
    curv = sum_all(s * c.astype(F32))
    return s, c, curv, res_norm, dir_norm, beta


def curv_kernel(*refs, n, first):
    parts, refs = refs[:n], refs[n:]
    s_prev, sc_prev = None, None
    if not first:
        (s_prev, sc_prev), refs = refs[:2], refs[2:]
    p_ref, scale_ref, x_ref, s_ref, c_ref, send0_ref, send1_ref, block_ref, sc_ref = refs
    s, c, curv, res_norm, dir_norm, beta = curvature(parts, s_prev, sc_prev, p_ref, scale_ref)
    s_ref[...] = s
    c_ref[...] = c
    sc_ref[0:1, :] = jnp.broadcast_to(res_norm, (1, LANES))
    sc_ref[1:2, :] = jnp.broadcast_to(dir_norm, (1, LANES))
    sc_ref[2:3, :] = jnp.broadcast_to(beta, (1, LANES))
    sc_ref[3:, :] = jnp.zeros((5, LANES), F32)
    block = scalar_block((curv,), lax.axis_index("dp"))
    block_ref[...] = block
    send_columns(c, x_ref, block, send0_ref, send1_ref)


def own_columns_kernel(*refs, part):
    c_ref, x_ref, out_ref = refs[0], refs[-2], refs[-1]
    if part == 0:
        out_ref[:, x_ref.shape[1] // 4 :] = refs[1][...]
    column_part(c_ref[...], x_ref, my_core(), part, out_ref)


def residual_out(residual, sums, aux_ref, send_ref):
    size = residual.shape[1]
    send_ref[:, :size] = residual.astype(BF16)
    if aux_ref is not None:
        for i, value in enumerate(sums):
            aux_ref[i : i + 1, :] = jnp.broadcast_to(value, (1, LANES))
    else:
        send_ref[:, size:] = scalar_block(sums, 0).astype(BF16)


def own_weight(w_ref, part, size):
    return w_ref[:, pl.ds(pl.multiple_of((2 * my_core() + part) * size, LANES), size)]


def gradient0_kernel(*refs, n):
    parts, (w_ref, weight_ref, r_ref, send_ref, aux_ref, scale_ref, loss_ref) = refs[:n], refs[n:]
    total = add_up(parts)
    size = r_ref.shape[1]
    block = total[:, size:]
    weight_total = read_scalar(block, 0)
    loss_ref[...] = jnp.broadcast_to(read_scalar(block, 1) / weight_total, loss_ref.shape)
    scale_ref[...] = one_row(weight_ref).astype(F32) / weight_total
    residual = -(total[:, :size] / weight_total + RIDGE_COEF * own_weight(w_ref, 0, size))
    r_ref[...] = residual
    aux_ref[...] = jnp.zeros(aux_ref.shape, F32)
    residual_out(residual, (sum_all(residual * residual), weight_total), aux_ref, send_ref)


def gradient1_kernel(*refs, n):
    parts, (w_ref, aux_ref, r_ref, send_ref) = refs[:n], refs[n:]
    total = add_up(parts)
    size = r_ref.shape[1]
    residual = -(total / aux_ref[1:2, 0:1] + RIDGE_COEF * own_weight(w_ref, 1, size))
    r_ref[...] = residual
    residual_out(residual, (aux_ref[0:1, 0:1] + sum_all(residual * residual),), None, send_ref)


def update_kernel(*refs, n, part, first, last):
    parts, refs = refs[:n], refs[n:]
    (r_ref, sc_ref, aux_ref), refs = refs[:3], refs[3:]
    direction = r_ref[...]
    if not first:
        direction = direction + sc_ref[2:3, 0:1] * refs[0][...]
        refs = refs[1:]
    if part == 0:
        send_ref, out_ref = refs[:2]
        refs = refs[2:]
    else:
        send_ref, refs = refs[0], refs[1:]
    total = add_up(parts)
    size = direction.shape[1]
    if part == 0:
        curv = read_scalar(total[:, size:], 0) + RIDGE_COEF * sc_ref[1:2, 0:1]
        alpha = sc_ref[0:1, 0:1] / curv
    else:
        alpha = aux_ref[2:3, 0:1]
    residual = r_ref[...] - alpha * (total[:, :size] + RIDGE_COEF * direction)
    if not last:
        r_out, d_out = refs
        r_out[...] = residual
        d_out[...] = direction
    sums = (sum_all(residual * residual), sum_all(residual * direction))
    if part == 0:
        out_ref[...] = jnp.zeros(out_ref.shape, F32)
        residual_out(residual, sums + (alpha,), out_ref, send_ref)
    else:
        sums = tuple(aux_ref[i : i + 1, 0:1] + value for i, value in enumerate(sums))
        residual_out(residual, sums, None, send_ref)


def row_blocks(xt_ref):
    rows = xt_ref.shape[1]
    width = math.gcd(rows, 512)
    return [slice(i, i + width) for i in range(0, rows, width)]


def row_part(h, xt_ref, which, part, block):
    size = xt_ref.shape[0] // 4
    at = pl.ds(pl.multiple_of((2 * which + part) * size, LANES), size)
    return lax.dot_general(h, xt_ref[at, block], NN, preferred_element_type=F32)


def rows0_kernel(mine0_ref, xt_ref, out_ref):
    h = mine0_ref[...]
    for block in row_blocks(xt_ref):
        out_ref[:, block] = row_part(h, xt_ref, my_core(), 0, block)


def rows1_kernel(acc_ref, mine1_ref, recv0_ref, xt_ref, out_ref):
    mine, mate = mine1_ref[:, : xt_ref.shape[0] // 4], recv0_ref[...]
    for block in row_blocks(xt_ref):
        out_ref[:, block] = (
            acc_ref[:, block]
            + row_part(mine, xt_ref, my_core(), 1, block)
            + row_part(mate, xt_ref, 1 - my_core(), 0, block)
        )


def rows2_kernel(acc_ref, mine1_ref, recv1_ref, xt_ref, out_ref):
    size, rows = xt_ref.shape[0] // 4, xt_ref.shape[1]
    h = recv1_ref[:, :size]
    both = mine1_ref[:, size:].astype(F32) + recv1_ref[:, size:].astype(F32)
    out_ref[:, rows:] = scalar_block(
        (read_scalar(both, 0), read_scalar(both, 1)), lax.axis_index("feat")
    ).astype(BF16)
    for block in row_blocks(xt_ref):
        part = acc_ref[:, block] + row_part(h, xt_ref, 1 - my_core(), 1, block)
        out_ref[:, block] = part.astype(BF16)


def last_kernel(*refs, n):
    parts, (s_prev, sc_prev, p_ref, scale_ref, s_ref, curv_ref) = refs[:n], refs[n:]
    s, c, curv, res_norm, dir_norm, beta = curvature(parts, s_prev, sc_prev, p_ref, scale_ref)
    s_ref[...] = s
    curv_ref[0:1, :] = jnp.broadcast_to(curv, (1, LANES))
    curv_ref[1:2, :] = jnp.broadcast_to(dir_norm, (1, LANES))
    curv_ref[2:3, :] = jnp.broadcast_to(res_norm, (1, LANES))
    curv_ref[3:, :] = jnp.zeros((5, LANES), F32)


def finish_kernel(*refs, n):
    parts, (sc_ref, loss_ref), refs = refs[:n], refs[n : n + 2], refs[n + 2 :]
    curv = add_up(parts)
    count = (len(refs) - 2) // 2
    steps, scores, (out_ref, loss_out) = refs[:count], refs[count:-2], refs[-2:]
    loss_out[0, 0] = jnp.max(loss_ref[...])
    last = sc_ref[2:3, 0:1] / (curv[0:1, 0:1] + RIDGE_COEF * sc_ref[1:2, 0:1])
    total = last * scores[-1][...]
    for alpha, score in zip(steps, scores[:-1]):
        total += alpha[2:3, 0:1] * score[...]
    out_ref[...] = total


def add_kernel(*refs):
    refs[-1][...] = add_up(refs[:-1]).astype(refs[-1].dtype)


def call(kernel, name, outs, *args, pins=(), scratch=(), keep=(), out_space=pltpu.VMEM, out_specs=(), limit=VMEM_LIMIT):
    def body(*refs):
        kernel(*refs[: len(args)], *refs[len(args) + len(pins) :])

    args = tuple(
        pltpu.with_memory_space_constraint(a, pltpu.HBM) if i in keep else a
        for i, a in enumerate(args)
    )
    args_pins = args + tuple(pltpu.with_memory_space_constraint(p, pltpu.VMEM) for p in pins)
    specs = [
        pl.BlockSpec(memory_space=pltpu.HBM if i in keep else pltpu.VMEM)
        for i in range(len(args_pins))
    ]
    return pl.pallas_call(
        body,
        out_shape=tuple(out_space(shape, dtype) for shape, dtype in outs),
        in_specs=specs,
        out_specs=tuple(pl.BlockSpec(memory_space=m) for m in out_specs or [pltpu.VMEM] * len(outs)),
        scratch_shapes=scratch,
        compiler_params=pltpu.CompilerParams(vmem_limit_bytes=limit),
        name=name,
    )(*args_pins)


def add(pins, *values, kind):
    return call(add_kernel, "add", [(values[0].shape, kind)], *values, pins=pins)[0]


def swap(value, axis, size, bit):
    return lax.ppermute(value, axis, [(i, i ^ bit) for i in range(size)])


def gather_sum(value, pins, axis, size, bits):
    kind = value.dtype
    if len(bits) > 2:
        a, b = bits[:2]
        value = add(
            pins, value, *[swap(value, axis, size, k) for k in (b, a, a | b)], kind=kind
        )
        bits = bits[2:]
    while len(bits) > 2:
        value = add(pins, value, swap(value, axis, size, bits[0]), kind=kind)
        bits = bits[1:]
    if len(bits) == 1:
        return [value, swap(value, axis, size, bits[0])]
    a, b = bits
    return [value] + [swap(value, axis, size, k) for k in (a, a | b, b)]


def bits_of(size):
    return [1 << i for i in range(size.bit_length() - 1)]


def on_device(features, weight, labels, sample_weight, *, dp, feat):
    classes, columns = weight.shape
    rows = features.shape[0]
    size = columns // 4
    labels = labels.reshape(rows // LANES, LANES)
    row_weight = sample_weight.reshape(rows // LANES, LANES)
    across_feat = functools.partial(gather_sum, axis="feat", size=feat, bits=bits_of(feat))
    across_chips = functools.partial(gather_sum, axis="dp", size=dp, bits=bits_of(dp)[1:])

    def core_swap(value):
        return swap(value, "dp", dp, 1)

    step = math.gcd(rows, 256)
    x, xt, weight, logit_part = call(
        functools.partial(load_kernel, step=step, ahead=2),
        "load",
        [
            ((rows, columns), BF16),
            ((columns, rows), BF16),
            ((classes, columns), F32),
            ((classes, rows), F32),
        ],
        features,
        weight,
        scratch=(pltpu.SemaphoreType.DMA((rows // step,)), pltpu.SemaphoreType.DMA),
        keep=(0, 1),
        limit=VMEM_LIMIT,
    )
    pins = [x, xt, weight]

    def column_sums(c, send0, send1, block):
        received0, received1 = core_swap(send0), core_swap(send1)
        sums = []
        for part, received, extra in ((0, received0, (block,)), (1, received1, ())):
            (own,) = call(
                functools.partial(own_columns_kernel, part=part),
                "own_columns",
                [((classes, size + LANES * len(extra)), F32)],
                c,
                *extra,
                x,
                pins=pins,
            )
            sums.append(across_chips(add(pins, own, received, kind=BF16), pins))
        return sums

    full = [((classes, rows), F32)]

    def first_rows(send0):
        received0 = core_swap(send0)
        (acc,) = call(rows0_kernel, "rows_0", full, send0, xt, pins=pins)
        return acc, received0

    def row_sums(acc, received0, send1):
        received1 = core_swap(send1)
        (acc,) = call(rows1_kernel, "rows_1", full, acc, send1, received0, xt, pins=pins)
        (score,) = call(
            rows2_kernel,
            "rows_2",
            [((classes, rows + LANES), BF16)],
            acc,
            send1,
            received1,
            xt,
            pins=pins,
        )
        return across_feat(score, pins)

    curv_outs = [
        ((classes, rows), BF16),
        ((classes, size + LANES), BF16),
        ((classes, size), BF16),
        ((16, LANES), F32),
    ]
    aux_out = ((8, LANES), F32)
    parts = across_feat(logit_part, pins)
    prob, e, send0, send1, block = call(
        functools.partial(probs_kernel, n=len(parts)),
        "probs",
        [((classes, rows), F32)] + curv_outs,
        *parts,
        labels,
        row_weight,
        x,
        pins=pins,
    )
    parts0, parts1 = column_sums(e, send0, send1, block)
    residual0, send0, aux, scale, loss = call(
        functools.partial(gradient0_kernel, n=len(parts0)),
        "gradient_0",
        [((classes, size), F32), ((classes, size), BF16), aux_out, ((1, rows), F32), aux_out],
        *parts0,
        weight,
        row_weight,
        pins=pins,
    )
    acc, received0 = first_rows(send0)
    residual1, send1 = call(
        functools.partial(gradient1_kernel, n=len(parts1)),
        "gradient_1",
        [((classes, size), F32), ((classes, size + LANES), BF16)],
        *parts1,
        weight,
        aux,
        pins=pins + [acc, received0],
    )
    residuals = [residual0, residual1]
    directions = [(), ()]
    pins[2:] = residuals
    state, steps, scores = (), [], []
    for i in range(CG_ITERS - 1):
        parts = row_sums(acc, received0, send1)
        s, c, send0, send1, block, sc = call(
            functools.partial(curv_kernel, n=len(parts), first=i == 0),
            "curvature",
            [((classes, rows), F32)] + curv_outs + [((8, LANES), F32)],
            *parts,
            *state,
            prob,
            scale,
            x,
            pins=pins,
        )
        state = (s, sc)
        scores.append(s)
        both = column_sums(c, send0, send1, block)
        last = i == CG_ITERS - 2
        vectors = [((classes, size), F32)] * (0 if last else 2)
        send0, aux, *first_half = call(
            functools.partial(update_kernel, n=len(both[0]), part=0, first=i == 0, last=last),
            "update_0",
            [((classes, size), BF16), aux_out] + vectors,
            *both[0],
            residuals[0],
            sc,
            sc,
            *directions[0],
            pins=pins,
        )
        acc, received0 = first_rows(send0)
        send1, *second_half = call(
            functools.partial(update_kernel, n=len(both[1]), part=1, first=i == 0, last=last),
            "update_1",
            [((classes, size + LANES), BF16)] + vectors,
            *both[1],
            residuals[1],
            sc,
            aux,
            *directions[1],
            pins=pins + [acc, received0],
        )
        steps.append(aux)
        if not last:
            residuals = [first_half[0], second_half[0]]
            directions = [first_half[1:], second_half[1:]]
        pins[2:] = first_half + second_half
    parts = row_sums(acc, received0, send1)
    s, sc = call(
        functools.partial(last_kernel, n=len(parts)),
        "last",
        [((classes, rows), F32), ((8, LANES), F32)],
        *parts,
        *state,
        prob,
        scale,
        pins=pins,
    )
    scores.append(s)
    parts = gather_sum(sc, pins, "dp", dp, bits_of(dp))
    out, loss = call(
        functools.partial(finish_kernel, n=len(parts)),
        "finish",
        [((classes, rows), F32), ((1, 1), F32)],
        *parts,
        sc,
        loss,
        *steps,
        *scores,
        out_space=jax.ShapeDtypeStruct,
        out_specs=(pltpu.VMEM, pltpu.SMEM),
    )
    return out.T, loss.reshape(())


def solution(mesh):
    dp, feat = mesh.shape["dp"], mesh.shape["feat"]
    in_specs = (P("dp", "feat"), P(None, "feat"), P("dp"), P("dp"))
    out_specs = (P("dp", None), P())
    return jax.shard_map(
        functools.partial(on_device, dp=dp, feat=feat),
        mesh=mesh,
        in_specs=in_specs,
        out_specs=out_specs,
        check_vma=False,
    )
```

```python
import functools
import math

import jax
import jax.numpy as jnp
from jax import lax
from jax.sharding import PartitionSpec as P
import jax.experimental.pallas as pl
import jax.experimental.pallas.tpu as pltpu

CG_ITERS = 4
RIDGE_COEF = 0.1
NORM_GUARD = 1e-06
LANES = 128
VMEM_LIMIT = 4 * 2**20
TURNED = 3

F32 = jnp.float32
BF16 = jnp.bfloat16
NT = (((1,), (1,)), ((), ()))
NN = (((1,), (0,)), ((), ()))


def scalar_block(values, lane):
    rows = lax.broadcasted_iota(jnp.int32, (16, LANES), 0)
    lanes = lax.broadcasted_iota(jnp.int32, (16, LANES), 1)
    block = jnp.zeros((16, LANES), F32)
    for i, value in enumerate(values):
        rest = jnp.broadcast_to(value, (16, LANES))
        for part in range(3):
            piece = rest.astype(BF16).astype(F32)
            block = jnp.where(rows == 3 * i + part, piece, block)
            rest = rest - piece
    return jnp.where(lanes == lane, block, 0.0)


def read_scalar(block, i):
    rows = lax.broadcasted_iota(jnp.int32, (16, LANES), 0)
    mine = (rows >= 3 * i) & (rows < 3 * i + 3)
    return jnp.sum(jnp.where(mine, block, 0.0), keepdims=True)


def sum_all(value):
    return jnp.sum(value, keepdims=True)


def one_row(ref):
    return jnp.concatenate([ref[i : i + 1, :] for i in range(ref.shape[0])], axis=1)


def add_up(parts):
    values = [p[...].astype(F32) for p in parts]
    while len(values) > 1:
        values = [a + b for a, b in zip(values[::2], values[1::2])]
    return values[0]


def my_core():
    return lax.rem(lax.axis_index("dp"), 2)


def load_kernel(x_hbm, w_hbm, x_ref, xt_ref, w_ref, l_ref, sems, w_sem, *, step, ahead):
    rows, columns = x_ref.shape
    chunks = rows // step
    block = math.gcd(columns, 512)

    def rows_of(i):
        return pl.ds(pl.multiple_of(i * step, step), step)

    def copy(i):
        return pltpu.make_async_copy(x_hbm.at[rows_of(i)], x_ref.at[rows_of(i)], sems.at[i])

    w_copy = pltpu.make_async_copy(w_hbm, w_ref, w_sem)
    w_copy.start()
    for i in range(min(ahead, chunks)):
        copy(i).start()
    w_copy.wait()

    @pl.loop(0, chunks)
    def _(i):
        copy(i).wait()

        @pl.when(i + ahead < chunks)
        def _():
            copy(i + ahead).start()

        total = jnp.zeros((w_ref.shape[0], step), F32)
        for j in range(0, columns, block):
            turned = x_ref[rows_of(i), j : j + block].T
            xt_ref[j : j + block, rows_of(i)] = turned
            w = w_ref[:, j : j + block].astype(BF16)
            total += lax.dot_general(w, turned, NN, preferred_element_type=F32)
        l_ref[:, rows_of(i)] = total


def column_part(c, x_ref, which, part, out_ref):
    size = x_ref.shape[1] // 4
    width = math.gcd(size, 512)
    for i in range(0, size, width):
        cols = pl.ds(pl.multiple_of((2 * which + part) * size + i, LANES), width)
        block = lax.dot_general(c, x_ref[:, cols], NN, preferred_element_type=F32)
        out_ref[:, i : i + width] = block.astype(out_ref.dtype)


def send_columns(c, x_ref, block, send0_ref):
    send0_ref[:, x_ref.shape[1] // 4 :] = block.astype(BF16)
    column_part(c, x_ref, 1 - my_core(), 0, send0_ref)


def mate_columns_kernel(c_ref, x_ref, send1_ref):
    column_part(c_ref[...], x_ref, 1 - my_core(), 1, send1_ref)


def probs_kernel(*refs, n):
    parts, refs = refs[:n], refs[n:]
    labels_ref, weight_ref, x_ref, p_ref, e_ref, send0_ref, block_ref = refs
    logits = add_up(parts)
    classes = logits.shape[0]
    top = jnp.max(logits, axis=0, keepdims=True)
    shifted = jnp.exp(logits - top)
    summed = jnp.sum(shifted, axis=0, keepdims=True)
    prob = shifted / summed
    log_total = top + jnp.log(summed)
    row_weight = one_row(weight_ref).astype(F32)
    rows = lax.broadcasted_iota(jnp.int32, logits.shape, 0)
    onehot = (rows == one_row(labels_ref)).astype(F32)
    picked = jnp.sum(logits * onehot, axis=0, keepdims=True)
    p_ref[...] = prob
    e = (row_weight * (prob - onehot)).astype(BF16)
    e_ref[...] = e
    block = scalar_block(
        (sum_all(row_weight), sum_all(row_weight * (log_total - picked))), lax.axis_index("dp")
    )
    block_ref[...] = block
    send_columns(e, x_ref, block, send0_ref)


def curvature(parts, s_prev, sc_prev, p_ref, scale_ref):
    total = add_up(parts)
    rows = p_ref.shape[1]
    block = total[:, rows:]
    u = total[:, :rows]
    res_norm = read_scalar(block, 0)
    if s_prev is None:
        beta = jnp.zeros((1, 1), F32)
        s = u
        dir_norm = res_norm
    else:
        cross = read_scalar(block, 1)
        beta = res_norm / (sc_prev[0:1, 0:1] + NORM_GUARD)
        s = u + beta * s_prev[...]
        dir_norm = res_norm + 2.0 * beta * cross + beta * beta * sc_prev[1:2, 0:1]
    prob = p_ref[...]
    mixed = jnp.sum(prob * s, axis=0, keepdims=True)
    c = (scale_ref[...] * prob * (s - mixed)).astype(BF16)
    curv = sum_all(s * c.astype(F32))
    return s, c, curv, res_norm, dir_norm, beta


def curv_kernel(*refs, n, first):
    parts, refs = refs[:n], refs[n:]
    s_prev, sc_prev = None, None
    if not first:
        (s_prev, sc_prev), refs = refs[:2], refs[2:]
    p_ref, scale_ref, x_ref, s_ref, c_ref, send0_ref, block_ref, sc_ref = refs
    s, c, curv, res_norm, dir_norm, beta = curvature(parts, s_prev, sc_prev, p_ref, scale_ref)
    s_ref[...] = s
    c_ref[...] = c
    sc_ref[0:1, :] = jnp.broadcast_to(res_norm, (1, LANES))
    sc_ref[1:2, :] = jnp.broadcast_to(dir_norm, (1, LANES))
    sc_ref[2:3, :] = jnp.broadcast_to(beta, (1, LANES))
    sc_ref[3:, :] = jnp.zeros((5, LANES), F32)
    block = scalar_block((curv,), lax.axis_index("dp"))
    block_ref[...] = block
    send_columns(c, x_ref, block, send0_ref)


def own_columns_kernel(*refs, part):
    c_ref, x_ref, out_ref = refs[0], refs[-2], refs[-1]
    if part == 0:
        out_ref[:, x_ref.shape[1] // 4 :] = refs[1][...]
    column_part(c_ref[...], x_ref, my_core(), part, out_ref)


def residual_out(residual, sums, aux_ref, send_ref):
    size = residual.shape[1]
    send_ref[:, :size] = residual.astype(BF16)
    if aux_ref is not None:
        for i, value in enumerate(sums):
            aux_ref[i : i + 1, :] = jnp.broadcast_to(value, (1, LANES))
    else:
        send_ref[:, size:] = scalar_block(sums, 0).astype(BF16)


def own_weight(w_ref, part, size):
    return w_ref[:, pl.ds(pl.multiple_of((2 * my_core() + part) * size, LANES), size)]


def gradient0_kernel(*refs, n):
    parts, (w_ref, weight_ref, r_ref, send_ref, aux_ref, scale_ref, loss_ref) = refs[:n], refs[n:]
    total = add_up(parts)
    size = r_ref.shape[1]
    block = total[:, size:]
    weight_total = read_scalar(block, 0)
    loss_ref[...] = jnp.broadcast_to(read_scalar(block, 1) / weight_total, loss_ref.shape)
    scale_ref[...] = one_row(weight_ref).astype(F32) / weight_total
    residual = -(total[:, :size] / weight_total + RIDGE_COEF * own_weight(w_ref, 0, size))
    r_ref[...] = residual
    aux_ref[...] = jnp.zeros(aux_ref.shape, F32)
    residual_out(residual, (sum_all(residual * residual), weight_total), aux_ref, send_ref)


def gradient1_kernel(*refs, n):
    parts, (w_ref, aux_ref, r_ref, send_ref) = refs[:n], refs[n:]
    total = add_up(parts)
    size = r_ref.shape[1]
    residual = -(total / aux_ref[1:2, 0:1] + RIDGE_COEF * own_weight(w_ref, 1, size))
    r_ref[...] = residual
    residual_out(residual, (aux_ref[0:1, 0:1] + sum_all(residual * residual),), None, send_ref)


def update_kernel(*refs, n, part, first, last):
    parts, refs = refs[:n], refs[n:]
    (r_ref, sc_ref, aux_ref), refs = refs[:3], refs[3:]
    direction = r_ref[...]
    if not first:
        direction = direction + sc_ref[2:3, 0:1] * refs[0][...]
        refs = refs[1:]
    if part == 0:
        send_ref, out_ref = refs[:2]
        refs = refs[2:]
    else:
        send_ref, refs = refs[0], refs[1:]
    total = add_up(parts)
    size = direction.shape[1]
    if part == 0:
        curv = read_scalar(total[:, size:], 0) + RIDGE_COEF * sc_ref[1:2, 0:1]
        alpha = sc_ref[0:1, 0:1] / curv
    else:
        alpha = aux_ref[2:3, 0:1]
    residual = r_ref[...] - alpha * (total[:, :size] + RIDGE_COEF * direction)
    if not last:
        r_out, d_out = refs
        r_out[...] = residual
        d_out[...] = direction
    sums = (sum_all(residual * residual), sum_all(residual * direction))
    if part == 0:
        out_ref[...] = jnp.zeros(out_ref.shape, F32)
        residual_out(residual, sums + (alpha,), out_ref, send_ref)
    else:
        sums = tuple(aux_ref[i : i + 1, 0:1] + value for i, value in enumerate(sums))
        residual_out(residual, sums, None, send_ref)


def row_blocks(xt_ref):
    rows = xt_ref.shape[1]
    width = math.gcd(rows, 512)
    return [slice(i, i + width) for i in range(0, rows, width)]


def row_part(h, xt_ref, which, part, block):
    size = xt_ref.shape[0] // 4
    at = pl.ds(pl.multiple_of((2 * which + part) * size, LANES), size)
    return lax.dot_general(h, xt_ref[at, block], NN, preferred_element_type=F32)


def rows0_kernel(mine0_ref, xt_ref, out_ref):
    h = mine0_ref[...]
    for block in row_blocks(xt_ref):
        out_ref[:, block] = row_part(h, xt_ref, my_core(), 0, block)


def rows1_kernel(acc_ref, mine1_ref, recv0_ref, xt_ref, out_ref):
    mine, mate = mine1_ref[:, : xt_ref.shape[0] // 4], recv0_ref[...]
    for block in row_blocks(xt_ref):
        out_ref[:, block] = (
            acc_ref[:, block]
            + row_part(mine, xt_ref, my_core(), 1, block)
            + row_part(mate, xt_ref, 1 - my_core(), 0, block)
        )


def rows2_kernel(acc_ref, mine1_ref, recv1_ref, xt_ref, out_ref):
    size, rows = xt_ref.shape[0] // 4, xt_ref.shape[1]
    h = recv1_ref[:, :size]
    both = mine1_ref[:, size:].astype(F32) + recv1_ref[:, size:].astype(F32)
    out_ref[:, rows:] = scalar_block(
        (read_scalar(both, 0), read_scalar(both, 1)), lax.axis_index("feat")
    ).astype(BF16)
    for block in row_blocks(xt_ref):
        part = acc_ref[:, block] + row_part(h, xt_ref, 1 - my_core(), 1, block)
        out_ref[:, block] = part.astype(BF16)


def last_kernel(*refs, n):
    parts, (s_prev, sc_prev, p_ref, scale_ref, s_ref, curv_ref) = refs[:n], refs[n:]
    s, c, curv, res_norm, dir_norm, beta = curvature(parts, s_prev, sc_prev, p_ref, scale_ref)
    s_ref[...] = s
    curv_ref[0:1, :] = jnp.broadcast_to(curv, (1, LANES))
    curv_ref[1:2, :] = jnp.broadcast_to(dir_norm, (1, LANES))
    curv_ref[2:3, :] = jnp.broadcast_to(res_norm, (1, LANES))
    curv_ref[3:, :] = jnp.zeros((5, LANES), F32)


def finish_kernel(*refs, n):
    parts, (sc_ref, loss_ref), refs = refs[:n], refs[n : n + 2], refs[n + 2 :]
    curv = add_up(parts)
    count = (len(refs) - 2) // 2
    steps, scores, (out_ref, loss_out) = refs[:count], refs[count:-2], refs[-2:]
    loss_out[0, 0] = jnp.max(loss_ref[...])
    last = sc_ref[2:3, 0:1] / (curv[0:1, 0:1] + RIDGE_COEF * sc_ref[1:2, 0:1])
    total = last * scores[-1][...]
    for alpha, score in zip(steps, scores[:-1]):
        total += alpha[2:3, 0:1] * score[...]
    out_ref[...] = total


def add_kernel(*refs):
    refs[-1][...] = add_up(refs[:-1]).astype(refs[-1].dtype)


def call(kernel, name, outs, *args, pins=(), scratch=(), keep=(), out_space=pltpu.VMEM, out_specs=(), limit=VMEM_LIMIT):
    def body(*refs):
        kernel(*refs[: len(args)], *refs[len(args) + len(pins) :])

    args = tuple(
        pltpu.with_memory_space_constraint(a, pltpu.HBM) if i in keep else a
        for i, a in enumerate(args)
    )
    args_pins = args + tuple(pltpu.with_memory_space_constraint(p, pltpu.VMEM) for p in pins)
    specs = [
        pl.BlockSpec(memory_space=pltpu.HBM if i in keep else pltpu.VMEM)
        for i in range(len(args_pins))
    ]
    return pl.pallas_call(
        body,
        out_shape=tuple(out_space(shape, dtype) for shape, dtype in outs),
        in_specs=specs,
        out_specs=tuple(pl.BlockSpec(memory_space=m) for m in out_specs or [pltpu.VMEM] * len(outs)),
        scratch_shapes=scratch,
        compiler_params=pltpu.CompilerParams(vmem_limit_bytes=limit),
        name=name,
    )(*args_pins)


def add(pins, *values, kind):
    return call(add_kernel, "add", [(values[0].shape, kind)], *values, pins=pins)[0]


def swap(value, axis, size, bit):
    return lax.ppermute(value, axis, [(i, i ^ bit) for i in range(size)])


def gather_sum(value, pins, axis, size, bits):
    kind = value.dtype
    if len(bits) > 2:
        a, b = bits[:2]
        value = add(
            pins, value, *[swap(value, axis, size, k) for k in (b, a, a | b)], kind=kind
        )
        bits = bits[2:]
    while len(bits) > 2:
        value = add(pins, value, swap(value, axis, size, bits[0]), kind=kind)
        bits = bits[1:]
    if len(bits) == 1:
        return [value, swap(value, axis, size, bits[0])]
    a, b = bits
    return [value] + [swap(value, axis, size, k) for k in (a, a | b, b)]


def bits_of(size):
    return [1 << i for i in range(size.bit_length() - 1)]


def on_device(features, weight, labels, sample_weight, *, dp, feat):
    classes, columns = weight.shape
    rows = features.shape[0]
    size = columns // 4
    labels = labels.reshape(rows // LANES, LANES)
    row_weight = sample_weight.reshape(rows // LANES, LANES)
    across_feat = functools.partial(gather_sum, axis="feat", size=feat, bits=bits_of(feat))
    across_chips = functools.partial(gather_sum, axis="dp", size=dp, bits=bits_of(dp)[1:])

    def core_swap(value):
        return swap(value, "dp", dp, 1)

    step = math.gcd(rows, 256)
    x, xt, weight, logit_part = call(
        functools.partial(load_kernel, step=step, ahead=2),
        "load",
        [
            ((rows, columns), BF16),
            ((columns, rows), BF16),
            ((classes, columns), F32),
            ((classes, rows), F32),
        ],
        features,
        weight,
        scratch=(pltpu.SemaphoreType.DMA((rows // step,)), pltpu.SemaphoreType.DMA),
        keep=(0, 1),
        limit=VMEM_LIMIT,
    )
    pins = [x, xt, weight]

    def column_sums(c, send0, block):
        received0 = core_swap(send0)
        (send1,) = call(
            mate_columns_kernel, "mate_columns", [((classes, size), BF16)], c, x, pins=pins
        )
        received1 = core_swap(send1)
        sums = []
        for part, received, extra, after in ((0, received0, (block,), [send1]), (1, received1, (), [])):
            (own,) = call(
                functools.partial(own_columns_kernel, part=part),
                "own_columns",
                [((classes, size + LANES * len(extra)), F32)],
                c,
                *extra,
                x,
                pins=pins + after,
            )
            sums.append(across_chips(add(pins, own, received, kind=BF16), pins))
        return sums

    full = [((classes, rows), F32)]

    def first_rows(send0):
        received0 = core_swap(send0)
        (acc,) = call(rows0_kernel, "rows_0", full, send0, xt, pins=pins)
        return acc, received0

    def row_sums(acc, received0, send1):
        received1 = core_swap(send1)
        (acc,) = call(rows1_kernel, "rows_1", full, acc, send1, received0, xt, pins=pins)
        (score,) = call(
            rows2_kernel,
            "rows_2",
            [((classes, rows + LANES), BF16)],
            acc,
            send1,
            received1,
            xt,
            pins=pins,
        )
        return across_feat(score, pins)

    curv_outs = [
        ((classes, rows), BF16),
        ((classes, size + LANES), BF16),
        ((16, LANES), F32),
    ]
    aux_out = ((8, LANES), F32)
    parts = across_feat(logit_part, pins)
    prob, e, send0, block = call(
        functools.partial(probs_kernel, n=len(parts)),
        "probs",
        [((classes, rows), F32)] + curv_outs,
        *parts,
        labels,
        row_weight,
        x,
        pins=pins,
    )
    parts0, parts1 = column_sums(e, send0, block)
    residual0, send0, aux, scale, loss = call(
        functools.partial(gradient0_kernel, n=len(parts0)),
        "gradient_0",
        [((classes, size), F32), ((classes, size), BF16), aux_out, ((1, rows), F32), aux_out],
        *parts0,
        weight,
        row_weight,
        pins=pins,
    )
    acc, received0 = first_rows(send0)
    residual1, send1 = call(
        functools.partial(gradient1_kernel, n=len(parts1)),
        "gradient_1",
        [((classes, size), F32), ((classes, size + LANES), BF16)],
        *parts1,
        weight,
        aux,
        pins=pins + [acc, received0],
    )
    residuals = [residual0, residual1]
    directions = [(), ()]
    pins[2:] = residuals
    state, steps, scores = (), [], []
    for i in range(CG_ITERS - 1):
        parts = row_sums(acc, received0, send1)
        s, c, send0, block, sc = call(
            functools.partial(curv_kernel, n=len(parts), first=i == 0),
            "curvature",
            [((classes, rows), F32)] + curv_outs + [((8, LANES), F32)],
            *parts,
            *state,
            prob,
            scale,
            x,
            pins=pins,
        )
        state = (s, sc)
        scores.append(s)
        both = column_sums(c, send0, block)
        last = i == CG_ITERS - 2
        vectors = [((classes, size), F32)] * (0 if last else 2)
        send0, aux, *first_half = call(
            functools.partial(update_kernel, n=len(both[0]), part=0, first=i == 0, last=last),
            "update_0",
            [((classes, size), BF16), aux_out] + vectors,
            *both[0],
            residuals[0],
            sc,
            sc,
            *directions[0],
            pins=pins,
        )
        acc, received0 = first_rows(send0)
        send1, *second_half = call(
            functools.partial(update_kernel, n=len(both[1]), part=1, first=i == 0, last=last),
            "update_1",
            [((classes, size + LANES), BF16)] + vectors,
            *both[1],
            residuals[1],
            sc,
            aux,
            *directions[1],
            pins=pins + [acc, received0],
        )
        steps.append(aux)
        if not last:
            residuals = [first_half[0], second_half[0]]
            directions = [first_half[1:], second_half[1:]]
        pins[2:] = first_half + second_half
    parts = row_sums(acc, received0, send1)
    s, sc = call(
        functools.partial(last_kernel, n=len(parts)),
        "last",
        [((classes, rows), F32), ((8, LANES), F32)],
        *parts,
        *state,
        prob,
        scale,
        pins=pins,
    )
    scores.append(s)
    parts = gather_sum(sc, pins, "dp", dp, bits_of(dp))
    out, loss = call(
        functools.partial(finish_kernel, n=len(parts)),
        "finish",
        [((classes, rows), F32), ((1, 1), F32)],
        *parts,
        sc,
        loss,
        *steps,
        *scores,
        out_space=jax.ShapeDtypeStruct,
        out_specs=(pltpu.VMEM, pltpu.SMEM),
    )
    return out.T, loss.reshape(())


def solution(mesh):
    dp, feat = mesh.shape["dp"], mesh.shape["feat"]
    in_specs = (P("dp", "feat"), P(None, "feat"), P("dp"), P("dp"))
    out_specs = (P("dp", None), P())
    return jax.shard_map(
        functools.partial(on_device, dp=dp, feat=feat),
        mesh=mesh,
        in_specs=in_specs,
        out_specs=out_specs,
        check_vma=False,
    )
```

```python
import functools
import math

import jax
import jax.numpy as jnp
from jax import lax
from jax.sharding import PartitionSpec as P
import jax.experimental.pallas as pl
import jax.experimental.pallas.tpu as pltpu

CG_ITERS = 4
RIDGE_COEF = 0.1
NORM_GUARD = 1e-06
LANES = 128
VMEM_LIMIT = 4 * 2**20
TURNED = 3

F32 = jnp.float32
BF16 = jnp.bfloat16
NT = (((1,), (1,)), ((), ()))
NN = (((1,), (0,)), ((), ()))


def scalar_block(values, lane):
    rows = lax.broadcasted_iota(jnp.int32, (16, LANES), 0)
    lanes = lax.broadcasted_iota(jnp.int32, (16, LANES), 1)
    block = jnp.zeros((16, LANES), F32)
    for i, value in enumerate(values):
        rest = jnp.broadcast_to(value, (16, LANES))
        for part in range(3):
            piece = rest.astype(BF16).astype(F32)
            block = jnp.where(rows == 3 * i + part, piece, block)
            rest = rest - piece
    return jnp.where(lanes == lane, block, 0.0)


def read_scalar(block, i):
    rows = lax.broadcasted_iota(jnp.int32, (16, LANES), 0)
    mine = (rows >= 3 * i) & (rows < 3 * i + 3)
    return jnp.sum(jnp.where(mine, block, 0.0), keepdims=True)


def sum_all(value):
    return jnp.sum(value, keepdims=True)


def one_row(ref):
    return jnp.concatenate([ref[i : i + 1, :] for i in range(ref.shape[0])], axis=1)


def add_up(parts):
    values = [p[...].astype(F32) for p in parts]
    while len(values) > 1:
        values = [a + b for a, b in zip(values[::2], values[1::2])]
    return values[0]


def my_core():
    return lax.rem(lax.axis_index("dp"), 2)


def load_kernel(x_hbm, w_hbm, x_ref, xt_ref, w_ref, l_ref, sems, w_sem, *, step, ahead):
    rows, columns = x_ref.shape
    chunks = rows // step
    block = math.gcd(columns, 1024)

    def rows_of(i):
        return pl.ds(pl.multiple_of(i * step, step), step)

    def copy(i):
        return pltpu.make_async_copy(x_hbm.at[rows_of(i)], x_ref.at[rows_of(i)], sems.at[i])

    w_copy = pltpu.make_async_copy(w_hbm, w_ref, w_sem)
    w_copy.start()
    for i in range(min(ahead, chunks)):
        copy(i).start()
    w_copy.wait()

    @pl.loop(0, chunks)
    def _(i):
        copy(i).wait()

        @pl.when(i + ahead < chunks)
        def _():
            copy(i + ahead).start()

        total = jnp.zeros((w_ref.shape[0], step), F32)
        for j in range(0, columns, block):
            turned = x_ref[rows_of(i), j : j + block].T
            xt_ref[j : j + block, rows_of(i)] = turned
            w = w_ref[:, j : j + block].astype(BF16)
            total += lax.dot_general(w, turned, NN, preferred_element_type=F32)
        l_ref[:, rows_of(i)] = total


def column_part(c, x_ref, which, part, out_ref):
    size = x_ref.shape[1] // 4
    width = math.gcd(size, 512)
    for i in range(0, size, width):
        cols = pl.ds(pl.multiple_of((2 * which + part) * size + i, LANES), width)
        block = lax.dot_general(c, x_ref[:, cols], NN, preferred_element_type=F32)
        out_ref[:, i : i + width] = block.astype(out_ref.dtype)


def send_columns(c, x_ref, block, send0_ref):
    send0_ref[:, x_ref.shape[1] // 4 :] = block.astype(BF16)
    column_part(c, x_ref, 1 - my_core(), 0, send0_ref)


def mate_columns_kernel(c_ref, x_ref, send1_ref):
    column_part(c_ref[...], x_ref, 1 - my_core(), 1, send1_ref)


def probs_kernel(*refs, n):
    parts, refs = refs[:n], refs[n:]
    labels_ref, weight_ref, x_ref, p_ref, e_ref, send0_ref, block_ref = refs
    logits = add_up(parts)
    classes = logits.shape[0]
    top = jnp.max(logits, axis=0, keepdims=True)
    shifted = jnp.exp(logits - top)
    summed = jnp.sum(shifted, axis=0, keepdims=True)
    prob = shifted / summed
    log_total = top + jnp.log(summed)
    row_weight = one_row(weight_ref).astype(F32)
    rows = lax.broadcasted_iota(jnp.int32, logits.shape, 0)
    onehot = (rows == one_row(labels_ref)).astype(F32)
    picked = jnp.sum(logits * onehot, axis=0, keepdims=True)
    p_ref[...] = prob
    e = (row_weight * (prob - onehot)).astype(BF16)
    e_ref[...] = e
    block = scalar_block(
        (sum_all(row_weight), sum_all(row_weight * (log_total - picked))), lax.axis_index("dp")
    )
    block_ref[...] = block
    send_columns(e, x_ref, block, send0_ref)


def curvature(parts, s_prev, sc_prev, p_ref, scale_ref):
    total = add_up(parts)
    rows = p_ref.shape[1]
    block = total[:, rows:]
    u = total[:, :rows]
    res_norm = read_scalar(block, 0)
    if s_prev is None:
        beta = jnp.zeros((1, 1), F32)
        s = u
        dir_norm = res_norm
    else:
        cross = read_scalar(block, 1)
        beta = res_norm / (sc_prev[0:1, 0:1] + NORM_GUARD)
        s = u + beta * s_prev[...]
        dir_norm = res_norm + 2.0 * beta * cross + beta * beta * sc_prev[1:2, 0:1]
    prob = p_ref[...]
    mixed = jnp.sum(prob * s, axis=0, keepdims=True)
    c = (scale_ref[...] * prob * (s - mixed)).astype(BF16)
    curv = sum_all(s * c.astype(F32))
    return s, c, curv, res_norm, dir_norm, beta


def curv_kernel(*refs, n, first):
    parts, refs = refs[:n], refs[n:]
    s_prev, sc_prev = None, None
    if not first:
        (s_prev, sc_prev), refs = refs[:2], refs[2:]
    p_ref, scale_ref, x_ref, s_ref, c_ref, send0_ref, block_ref, sc_ref = refs
    s, c, curv, res_norm, dir_norm, beta = curvature(parts, s_prev, sc_prev, p_ref, scale_ref)
    s_ref[...] = s
    c_ref[...] = c
    sc_ref[0:1, :] = jnp.broadcast_to(res_norm, (1, LANES))
    sc_ref[1:2, :] = jnp.broadcast_to(dir_norm, (1, LANES))
    sc_ref[2:3, :] = jnp.broadcast_to(beta, (1, LANES))
    sc_ref[3:, :] = jnp.zeros((5, LANES), F32)
    block = scalar_block((curv,), lax.axis_index("dp"))
    block_ref[...] = block
    send_columns(c, x_ref, block, send0_ref)


def own_columns_kernel(*refs, part):
    c_ref, x_ref, out_ref = refs[0], refs[-2], refs[-1]
    if part == 0:
        out_ref[:, x_ref.shape[1] // 4 :] = refs[1][...]
    column_part(c_ref[...], x_ref, my_core(), part, out_ref)


def residual_out(residual, sums, aux_ref, send_ref):
    size = residual.shape[1]
    send_ref[:, :size] = residual.astype(BF16)
    if aux_ref is not None:
        for i, value in enumerate(sums):
            aux_ref[i : i + 1, :] = jnp.broadcast_to(value, (1, LANES))
    else:
        send_ref[:, size:] = scalar_block(sums, 0).astype(BF16)


def own_weight(w_ref, part, size):
    return w_ref[:, pl.ds(pl.multiple_of((2 * my_core() + part) * size, LANES), size)]


def gradient0_kernel(*refs, n):
    parts, (w_ref, weight_ref, r_ref, send_ref, aux_ref, scale_ref, loss_ref) = refs[:n], refs[n:]
    total = add_up(parts)
    size = r_ref.shape[1]
    block = total[:, size:]
    weight_total = read_scalar(block, 0)
    loss_ref[...] = jnp.broadcast_to(read_scalar(block, 1) / weight_total, loss_ref.shape)
    scale_ref[...] = one_row(weight_ref).astype(F32) / weight_total
    residual = -(total[:, :size] / weight_total + RIDGE_COEF * own_weight(w_ref, 0, size))
    r_ref[...] = residual
    aux_ref[...] = jnp.zeros(aux_ref.shape, F32)
    residual_out(residual, (sum_all(residual * residual), weight_total), aux_ref, send_ref)


def gradient1_kernel(*refs, n):
    parts, (w_ref, aux_ref, r_ref, send_ref) = refs[:n], refs[n:]
    total = add_up(parts)
    size = r_ref.shape[1]
    residual = -(total / aux_ref[1:2, 0:1] + RIDGE_COEF * own_weight(w_ref, 1, size))
    r_ref[...] = residual
    residual_out(residual, (aux_ref[0:1, 0:1] + sum_all(residual * residual),), None, send_ref)


def update_kernel(*refs, n, part, first, last):
    parts, refs = refs[:n], refs[n:]
    (r_ref, sc_ref, aux_ref), refs = refs[:3], refs[3:]
    direction = r_ref[...]
    if not first:
        direction = direction + sc_ref[2:3, 0:1] * refs[0][...]
        refs = refs[1:]
    if part == 0:
        send_ref, out_ref = refs[:2]
        refs = refs[2:]
    else:
        send_ref, refs = refs[0], refs[1:]
    total = add_up(parts)
    size = direction.shape[1]
    if part == 0:
        curv = read_scalar(total[:, size:], 0) + RIDGE_COEF * sc_ref[1:2, 0:1]
        alpha = sc_ref[0:1, 0:1] / curv
    else:
        alpha = aux_ref[2:3, 0:1]
    residual = r_ref[...] - alpha * (total[:, :size] + RIDGE_COEF * direction)
    if not last:
        r_out, d_out = refs
        r_out[...] = residual
        d_out[...] = direction
    sums = (sum_all(residual * residual), sum_all(residual * direction))
    if part == 0:
        out_ref[...] = jnp.zeros(out_ref.shape, F32)
        residual_out(residual, sums + (alpha,), out_ref, send_ref)
    else:
        sums = tuple(aux_ref[i : i + 1, 0:1] + value for i, value in enumerate(sums))
        residual_out(residual, sums, None, send_ref)


def row_blocks(xt_ref):
    rows = xt_ref.shape[1]
    width = math.gcd(rows, 512)
    return [slice(i, i + width) for i in range(0, rows, width)]


def row_part(h, xt_ref, which, part, block):
    size = xt_ref.shape[0] // 4
    at = pl.ds(pl.multiple_of((2 * which + part) * size, LANES), size)
    return lax.dot_general(h, xt_ref[at, block], NN, preferred_element_type=F32)


def rows0_kernel(mine0_ref, xt_ref, out_ref):
    h = mine0_ref[...]
    for block in row_blocks(xt_ref):
        out_ref[:, block] = row_part(h, xt_ref, my_core(), 0, block)


def rows1_kernel(acc_ref, mine1_ref, recv0_ref, xt_ref, out_ref):
    mine, mate = mine1_ref[:, : xt_ref.shape[0] // 4], recv0_ref[...]
    for block in row_blocks(xt_ref):
        out_ref[:, block] = (
            acc_ref[:, block]
            + row_part(mine, xt_ref, my_core(), 1, block)
            + row_part(mate, xt_ref, 1 - my_core(), 0, block)
        )


def rows2_kernel(acc_ref, mine1_ref, recv1_ref, xt_ref, out_ref):
    size, rows = xt_ref.shape[0] // 4, xt_ref.shape[1]
    h = recv1_ref[:, :size]
    both = mine1_ref[:, size:].astype(F32) + recv1_ref[:, size:].astype(F32)
    out_ref[:, rows:] = scalar_block(
        (read_scalar(both, 0), read_scalar(both, 1)), lax.axis_index("feat")
    ).astype(BF16)
    for block in row_blocks(xt_ref):
        part = acc_ref[:, block] + row_part(h, xt_ref, 1 - my_core(), 1, block)
        out_ref[:, block] = part.astype(BF16)


def last_kernel(*refs, n):
    parts, (s_prev, sc_prev, p_ref, scale_ref, s_ref, curv_ref) = refs[:n], refs[n:]
    s, c, curv, res_norm, dir_norm, beta = curvature(parts, s_prev, sc_prev, p_ref, scale_ref)
    s_ref[...] = s
    curv_ref[0:1, :] = jnp.broadcast_to(curv, (1, LANES))
    curv_ref[1:2, :] = jnp.broadcast_to(dir_norm, (1, LANES))
    curv_ref[2:3, :] = jnp.broadcast_to(res_norm, (1, LANES))
    curv_ref[3:, :] = jnp.zeros((5, LANES), F32)


def finish_kernel(*refs, n):
    parts, (sc_ref, loss_ref), refs = refs[:n], refs[n : n + 2], refs[n + 2 :]
    curv = add_up(parts)
    count = (len(refs) - 2) // 2
    steps, scores, (out_ref, loss_out) = refs[:count], refs[count:-2], refs[-2:]
    loss_out[0, 0] = jnp.max(loss_ref[...])
    last = sc_ref[2:3, 0:1] / (curv[0:1, 0:1] + RIDGE_COEF * sc_ref[1:2, 0:1])
    total = last * scores[-1][...]
    for alpha, score in zip(steps, scores[:-1]):
        total += alpha[2:3, 0:1] * score[...]
    out_ref[...] = total


def add_kernel(*refs):
    refs[-1][...] = add_up(refs[:-1]).astype(refs[-1].dtype)


def call(kernel, name, outs, *args, pins=(), scratch=(), keep=(), out_space=pltpu.VMEM, out_specs=(), limit=VMEM_LIMIT):
    def body(*refs):
        kernel(*refs[: len(args)], *refs[len(args) + len(pins) :])

    args = tuple(
        pltpu.with_memory_space_constraint(a, pltpu.HBM) if i in keep else a
        for i, a in enumerate(args)
    )
    args_pins = args + tuple(pltpu.with_memory_space_constraint(p, pltpu.VMEM) for p in pins)
    specs = [
        pl.BlockSpec(memory_space=pltpu.HBM if i in keep else pltpu.VMEM)
        for i in range(len(args_pins))
    ]
    return pl.pallas_call(
        body,
        out_shape=tuple(out_space(shape, dtype) for shape, dtype in outs),
        in_specs=specs,
        out_specs=tuple(pl.BlockSpec(memory_space=m) for m in out_specs or [pltpu.VMEM] * len(outs)),
        scratch_shapes=scratch,
        compiler_params=pltpu.CompilerParams(vmem_limit_bytes=limit),
        name=name,
    )(*args_pins)


def add(pins, *values, kind):
    return call(add_kernel, "add", [(values[0].shape, kind)], *values, pins=pins)[0]


def swap(value, axis, size, bit):
    return lax.ppermute(value, axis, [(i, i ^ bit) for i in range(size)])


def gather_sum(value, pins, axis, size, bits):
    kind = value.dtype
    if len(bits) > 2:
        a, b = bits[:2]
        value = add(
            pins, value, *[swap(value, axis, size, k) for k in (b, a, a | b)], kind=kind
        )
        bits = bits[2:]
    while len(bits) > 2:
        value = add(pins, value, swap(value, axis, size, bits[0]), kind=kind)
        bits = bits[1:]
    if len(bits) == 1:
        return [value, swap(value, axis, size, bits[0])]
    a, b = bits
    return [value] + [swap(value, axis, size, k) for k in (a, a | b, b)]


def bits_of(size):
    return [1 << i for i in range(size.bit_length() - 1)]


def on_device(features, weight, labels, sample_weight, *, dp, feat):
    classes, columns = weight.shape
    rows = features.shape[0]
    size = columns // 4
    labels = labels.reshape(rows // LANES, LANES)
    row_weight = sample_weight.reshape(rows // LANES, LANES)
    across_feat = functools.partial(gather_sum, axis="feat", size=feat, bits=bits_of(feat))
    across_chips = functools.partial(gather_sum, axis="dp", size=dp, bits=bits_of(dp)[1:])

    def core_swap(value):
        return swap(value, "dp", dp, 1)

    step = math.gcd(rows, 256)
    x, xt, weight, logit_part = call(
        functools.partial(load_kernel, step=step, ahead=2),
        "load",
        [
            ((rows, columns), BF16),
            ((columns, rows), BF16),
            ((classes, columns), F32),
            ((classes, rows), F32),
        ],
        features,
        weight,
        scratch=(pltpu.SemaphoreType.DMA((rows // step,)), pltpu.SemaphoreType.DMA),
        keep=(0, 1),
        limit=VMEM_LIMIT,
    )
    pins = [x, xt, weight]

    def column_sums(c, send0, block):
        received0 = core_swap(send0)
        (send1,) = call(
            mate_columns_kernel, "mate_columns", [((classes, size), BF16)], c, x, pins=pins
        )
        received1 = core_swap(send1)
        sums = []
        for part, received, extra, after in ((0, received0, (block,), [send1]), (1, received1, (), [])):
            (own,) = call(
                functools.partial(own_columns_kernel, part=part),
                "own_columns",
                [((classes, size + LANES * len(extra)), F32)],
                c,
                *extra,
                x,
                pins=pins + after,
            )
            sums.append(across_chips(add(pins, own, received, kind=BF16), pins))
        return sums

    full = [((classes, rows), F32)]

    def first_rows(send0):
        received0 = core_swap(send0)
        (acc,) = call(rows0_kernel, "rows_0", full, send0, xt, pins=pins)
        return acc, received0

    def row_sums(acc, received0, send1):
        received1 = core_swap(send1)
        (acc,) = call(rows1_kernel, "rows_1", full, acc, send1, received0, xt, pins=pins)
        (score,) = call(
            rows2_kernel,
            "rows_2",
            [((classes, rows + LANES), BF16)],
            acc,
            send1,
            received1,
            xt,
            pins=pins,
        )
        return across_feat(score, pins)

    curv_outs = [
        ((classes, rows), BF16),
        ((classes, size + LANES), BF16),
        ((16, LANES), F32),
    ]
    aux_out = ((8, LANES), F32)
    parts = across_feat(logit_part, pins)
    prob, e, send0, block = call(
        functools.partial(probs_kernel, n=len(parts)),
        "probs",
        [((classes, rows), F32)] + curv_outs,
        *parts,
        labels,
        row_weight,
        x,
        pins=pins,
    )
    parts0, parts1 = column_sums(e, send0, block)
    residual0, send0, aux, scale, loss = call(
        functools.partial(gradient0_kernel, n=len(parts0)),
        "gradient_0",
        [((classes, size), F32), ((classes, size), BF16), aux_out, ((1, rows), F32), aux_out],
        *parts0,
        weight,
        row_weight,
        pins=pins,
    )
    acc, received0 = first_rows(send0)
    residual1, send1 = call(
        functools.partial(gradient1_kernel, n=len(parts1)),
        "gradient_1",
        [((classes, size), F32), ((classes, size + LANES), BF16)],
        *parts1,
        weight,
        aux,
        pins=pins + [acc, received0],
    )
    residuals = [residual0, residual1]
    directions = [(), ()]
    pins[2:] = residuals
    state, steps, scores = (), [], []
    for i in range(CG_ITERS - 1):
        parts = row_sums(acc, received0, send1)
        s, c, send0, block, sc = call(
            functools.partial(curv_kernel, n=len(parts), first=i == 0),
            "curvature",
            [((classes, rows), F32)] + curv_outs + [((8, LANES), F32)],
            *parts,
            *state,
            prob,
            scale,
            x,
            pins=pins,
        )
        state = (s, sc)
        scores.append(s)
        both = column_sums(c, send0, block)
        last = i == CG_ITERS - 2
        vectors = [((classes, size), F32)] * (0 if last else 2)
        send0, aux, *first_half = call(
            functools.partial(update_kernel, n=len(both[0]), part=0, first=i == 0, last=last),
            "update_0",
            [((classes, size), BF16), aux_out] + vectors,
            *both[0],
            residuals[0],
            sc,
            sc,
            *directions[0],
            pins=pins,
        )
        acc, received0 = first_rows(send0)
        send1, *second_half = call(
            functools.partial(update_kernel, n=len(both[1]), part=1, first=i == 0, last=last),
            "update_1",
            [((classes, size + LANES), BF16)] + vectors,
            *both[1],
            residuals[1],
            sc,
            aux,
            *directions[1],
            pins=pins + [acc, received0],
        )
        steps.append(aux)
        if not last:
            residuals = [first_half[0], second_half[0]]
            directions = [first_half[1:], second_half[1:]]
        pins[2:] = first_half + second_half
    parts = row_sums(acc, received0, send1)
    s, sc = call(
        functools.partial(last_kernel, n=len(parts)),
        "last",
        [((classes, rows), F32), ((8, LANES), F32)],
        *parts,
        *state,
        prob,
        scale,
        pins=pins,
    )
    scores.append(s)
    parts = gather_sum(sc, pins, "dp", dp, bits_of(dp))
    out, loss = call(
        functools.partial(finish_kernel, n=len(parts)),
        "finish",
        [((classes, rows), F32), ((1, 1), F32)],
        *parts,
        sc,
        loss,
        *steps,
        *scores,
        out_space=jax.ShapeDtypeStruct,
        out_specs=(pltpu.VMEM, pltpu.SMEM),
    )
    return out.T, loss.reshape(())


def solution(mesh):
    dp, feat = mesh.shape["dp"], mesh.shape["feat"]
    in_specs = (P("dp", "feat"), P(None, "feat"), P("dp"), P("dp"))
    out_specs = (P("dp", None), P())
    return jax.shard_map(
        functools.partial(on_device, dp=dp, feat=feat),
        mesh=mesh,
        in_specs=in_specs,
        out_specs=out_specs,
        check_vma=False,
    )
```
